128 devices in a mesh: section: 2 (over x_hi), pair: 2 (over x_lo), dp: 32 (over z, y, core).
Axes of the slice: x: 4 (x_hi: 2, x_lo: 2; x = x_hi * 2 + x_lo), y: 4, z: 4, core: 2. Of those that a mesh axis runs over, the one named last changes fastest.
Arguments:
- tokens: bfloat16 [2, 64, 128, 1280], P(None, ('pair', 'dp')), may hold values from -6 to 6
- lengths: int32 [2, 64], P(None, ('pair', 'dp')), may hold values from 32 to 128, as said below
- cotangent: bfloat16 [2, 64, 128, 1280], P(None, ('pair', 'dp')), may hold values from -6 to 6
- w_qkv: bfloat16 [2, 1280, 3840], P('section', 'pair'), may hold values from -0.15625 to 0.15625
- w_out: bfloat16 [2, 1280, 1280], P('section', 'pair'), may hold values from -0.625 to 0.625
- w_up: bfloat16 [2, 1280, 5120], P('section', 'pair'), may hold values from -0.15625 to 0.15625
- w_down: bfloat16 [2, 5120, 1280], P('section', 'pair'), may hold values from -0.078125 to 0.078125
- norm1_gain: float32 [2, 1280], P('section'), may hold values from 0.5 to 1.5
- norm1_bias: float32 [2, 1280], P('section'), may hold values from -3 to 3
- norm2_gain: float32 [2, 1280], P('section'), may hold values from 0.5 to 1.5
- norm2_bias: float32 [2, 1280], P('section'), may hold values from -3 to 3
Outputs:
- layer_outputs: bfloat16 [2, 2, 64, 128, 1280], P('section', None, ('pair', 'dp'))
- input_grads: bfloat16 [2, 2, 64, 128, 1280], P('section', None, ('pair', 'dp'))
- grad_qkv: float32 [2, 1280, 3840], P('section', ('pair', 'dp'))
- grad_out: float32 [2, 1280, 1280], P('section', ('pair', 'dp'))
- grad_up: float32 [2, 1280, 5120], P('section', ('pair', 'dp'))
- grad_down: float32 [2, 5120, 1280], P('section', ('pair', 'dp'))
- grad_norm1_gain: float32 [2, 1280], P('section', ('pair', 'dp'))
- grad_norm1_bias: float32 [2, 1280], P('section', ('pair', 'dp'))
- grad_norm2_gain: float32 [2, 1280], P('section', ('pair', 'dp'))
- grad_norm2_bias: float32 [2, 1280], P('section', ('pair', 'dp'))
The draws below stay inside these ranges and needn't reach their ends.
Inputs may be any that keep to these rules, and one draw needn't show every extreme that they name: `lengths`: in every micro-batch one sentence has length 128 and another 128 // 4.
All inputs are finite; a program needn't handle non-finite values.
Results may differ from the reference program's by a relative error of at most 0.017.
Values may be sent and summed in bfloat16 or wider, within the bound.
No kernel may reach another device: no remote copies, remote signals or barrier semaphores. Data moves between devices by JAX's collectives and lax.ppermute only.
A program may use at most 832 MiB of HBM per device.

```python
import jax
import jax.numpy as jnp
from jax import lax

D = 1280
HEADS = 20
FF = 5120
SEQ = 128
MICRO = 2
CELLS = 64


def draw_lengths(key, part):
    key = jax.random.fold_in(key, 11)
    draw_key, pick_key = jax.random.split(key)
    lengths_drawn = jax.random.randint(draw_key, (MICRO, CELLS), SEQ // 4, SEQ + 1, dtype=jnp.int32)
    shuffled = jax.random.permutation(pick_key, CELLS)
    micro_rows = jnp.arange(MICRO)
    lengths_drawn = lengths_drawn.at[micro_rows, shuffled[micro_rows]].set(SEQ)
    lengths_drawn = lengths_drawn.at[micro_rows, shuffled[micro_rows + MICRO]].set(SEQ // 4)
    return lengths_drawn.astype(jnp.int32)


def steps_of(key, dims, cuts, smallest, top_value):
    factor_of, own = 1.0, jax.random.fold_in(key, 6)
    for position, blocks in cuts:
        draws = jnp.exp(jax.random.uniform(jax.random.fold_in(own, position), (blocks,), jnp.float32, smallest / len(cuts), top_value / len(cuts)))
        factor_of = factor_of * jnp.repeat(draws, dims[position] // blocks).reshape([-1 if axis == position else 1 for axis in range(len(dims))])
    return factor_of


def bell_draw(key, extent, deviation, limit, pieces=(), kind=jnp.bfloat16):
    result = jax.random.normal(key, extent, jnp.float32) * deviation
    if len(pieces) > 0:
        result = steps_of(key, extent, pieces, -0.22, 0.18) * result
    return jnp.clip(result, min=-limit, max=limit).astype(kind)


def setup_inputs(seed: int = 0) -> dict:
    streams_of = jax.random.split(jax.random.key(seed), 12)
    return {
        "tokens": bell_draw(streams_of[0], (MICRO, CELLS, SEQ, D), 1.0, 6.0, ((1, 64),)),
        "lengths": draw_lengths(jax.random.fold_in(streams_of[11], 71), 0),
        "cotangent": bell_draw(streams_of[2], (MICRO, CELLS, SEQ, D), 1.0, 6.0, ((1, 64),)),
        "w_qkv": bell_draw(streams_of[3], (2, D, 3 * D), D ** -0.5, 0.15625, ((0, 2), (1, 2))),
        "w_out": bell_draw(streams_of[4], (2, D, D), (D // 16) ** -0.5, 0.625, ((0, 2), (1, 2))),
        "w_up": bell_draw(streams_of[5], (2, D, FF), D ** -0.5, 0.15625, ((0, 2), (1, 2))),
        "w_down": bell_draw(streams_of[6], (2, FF, D), FF ** -0.5, 0.078125, ((0, 2), (1, 2))),
        "norm1_gain": jnp.clip(1.0 + 0.1 * jax.random.normal(streams_of[7], (2, D), jnp.float32), 0.5, 1.5),
        "norm1_bias": bell_draw(streams_of[8], (2, D), 0.5, 3.0, ((0, 2),), jnp.float32),
        "norm2_gain": jnp.clip(1.0 + 0.1 * jax.random.normal(streams_of[9], (2, D), jnp.float32), 0.5, 1.5),
        "norm2_bias": bell_draw(streams_of[10], (2, D), 0.5, 3.0, ((0, 2),), jnp.float32),
    }


EPSILON = 1e-05
HIGH = lax.Precision.HIGHEST

@jax.custom_vjp
def low(v):
    return lax.optimization_barrier(v.astype(jnp.bfloat16)).astype(jnp.float32)

@jax.custom_vjp
def low_back(v):
    return v

def low_keep(v):
    return (low(v), None)

def low_pass(kept, grad):
    return (grad,)

def back_keep(v):
    return (v, None)

def back_low(kept, grad):
    return (low(grad),)
low.defvjp(low_keep, low_pass)
low_back.defvjp(back_keep, back_low)

def normalize(values, gain_row, bias_row):
    row_mean = lax.optimization_barrier(jnp.mean(values, axis=-1, keepdims=True))
    centred = values - row_mean
    variance = lax.optimization_barrier(jnp.mean(centred * centred, axis=-1, keepdims=True))
    return centred * lax.rsqrt(variance + EPSILON) * gain_row + bias_row

def encoder_layer(weights, inputs, keys_valid):
    w_qkv, w_out, w_up, w_down, gain_one, bias_one, gain_two, bias_two = weights
    seq_len = inputs.shape[0]
    head_dim = D // HEADS
    normed = low(normalize(inputs, gain_one, bias_one))
    qkv_all = low(low_back(jnp.dot(normed, w_qkv, precision=HIGH)))
    query_h = qkv_all[:, :D].reshape(seq_len, HEADS, head_dim)
    key_h = qkv_all[:, D:2 * D].reshape(seq_len, HEADS, head_dim)
    value_h = qkv_all[:, 2 * D:].reshape(seq_len, HEADS, head_dim)
    scores = jnp.einsum('qhd,khd->hqk', query_h, key_h, precision=HIGH) * head_dim ** (-0.5)
    scores = low_back(jnp.where(keys_valid[None, None, :], scores, -1e+30))
    attention = low(jax.nn.softmax(scores, axis=-1))
    mixed_all = jnp.einsum('hqk,khd->qhd', attention, value_h, precision=HIGH).reshape(seq_len, D)
    mixed_all = low(low_back(mixed_all))
    middle = inputs + low_back(jnp.dot(mixed_all, w_out, precision=HIGH))
    normed_two = low(normalize(middle, gain_two, bias_two))
    hidden = low_back(jnp.dot(normed_two, w_up, precision=HIGH))
    active = low(jax.nn.gelu(hidden, approximate=False))
    return middle + low_back(jnp.dot(active, w_down, precision=HIGH))

def reference(tokens, lengths, cotangent, w_qkv, w_out, w_up, w_down, norm1_gain, norm1_bias, norm2_gain, norm2_bias):
    weights = tuple((tensor.astype(jnp.float32) for tensor in (w_qkv, w_out, w_up, w_down, norm1_gain, norm1_bias, norm2_gain, norm2_bias)))
    sentence_count = MICRO * CELLS
    flat_tokens = tokens.reshape(sentence_count, SEQ, D)
    flat_lengths = lengths.reshape(sentence_count)
    flat_cot = cotangent.reshape(sentence_count, SEQ, D)

    def one_sentence(totals, sentence):
        token_rows, length_one, cot_rows = sentence
        keys_valid = jnp.arange(SEQ) < length_one

        def forward(params, inputs, probe):
            first_layer = tuple((tensor[0] for tensor in params))
            second_layer = tuple((tensor[1] for tensor in params))
            between = low(low_back(encoder_layer(first_layer, inputs, keys_valid) + probe))
            return (between, encoder_layer(second_layer, between, keys_valid))
        inputs = token_rows.astype(jnp.float32)
        probe = jnp.zeros((SEQ, D), jnp.float32)
        (between, final), pullback = jax.vjp(forward, weights, inputs, probe)
        grad_params, grad_inputs, grad_between = pullback((jnp.zeros_like(between), cot_rows.astype(jnp.float32)))
        totals = jax.tree.map(lambda total_part, new_part: total_part + new_part, totals, grad_params)
        return (totals, (between.astype(jnp.bfloat16), final.astype(jnp.bfloat16), grad_inputs.astype(jnp.bfloat16), grad_between.astype(jnp.bfloat16)))
    zero_grads = jax.tree.map(jnp.zeros_like, weights)
    totals, (betweens, finals, grad_first, grad_second) = lax.scan(one_sentence, zero_grads, (flat_tokens, flat_lengths, flat_cot))
    full_shape = (MICRO, CELLS, SEQ, D)
    layer_outputs = jnp.stack([betweens.reshape(full_shape), finals.reshape(full_shape)])
    input_grads = jnp.stack([grad_first.reshape(full_shape), grad_second.reshape(full_shape)])
    return (layer_outputs, input_grads, totals[0], totals[1], totals[2], totals[3], totals[4], totals[5], totals[6], totals[7])
```

```python
import functools

import jax
import jax.numpy as jnp
from jax import lax
from jax.experimental import pallas as pl
from jax.experimental.pallas import tpu as pltpu
from jax.sharding import PartitionSpec as P

D = 1280
FF = 5120
SEQ = 128
ROWS = 2 * SEQ
EPSILON = 1e-05
BF = jnp.bfloat16
F32 = jnp.float32
PIECE = 80

NN = (((1,), (0,)), ((), ()))
NT = (((1,), (1,)), ((), ()))
TN = (((0,), (0,)), ((), ()))


def dot(a, b, dims=NN):
    return lax.dot_general(a, b, dims, preferred_element_type=F32)


def row_blocks(count, body):
    def step(i, carry):
        body(pl.ds(pl.multiple_of(i * 32, 32), 32))
        return carry

    lax.fori_loop(0, count // 32, step, 0)


def stats(v):
    mean = jnp.mean(v, axis=-1, keepdims=True)
    centred = v - mean
    rstd = lax.rsqrt(jnp.mean(centred * centred, axis=-1, keepdims=True) + EPSILON)
    return centred * rstd, rstd


def start_square(pair, own, oth, which, dst, col, sem, group):
    pltpu.make_async_copy(
        own, dst.at[pl.ds(pl.multiple_of(pair * 640, 640), 640), pl.ds(col, D)], sem
    ).start()
    for r in range(8):
        row = pl.multiple_of((1 - pair) * 640 + r * PIECE, PIECE)
        pltpu.make_async_copy(
            oth.at[group * 8 + r, pl.ds(which * PIECE, PIECE)],
            dst.at[pl.ds(row, PIECE), pl.ds(col, D)],
            sem,
        ).start()


def start_tall(pair, own, oth, dst, sems):
    for u in range(2):
        pltpu.make_async_copy(
            own.at[pl.ds(u * D, D)],
            dst.at[pl.ds(pl.multiple_of(pair * 2560 + u * D, D), D)],
            sems.at[2 * pair + u],
        ).start()
    for d in range(32):
        row = pl.multiple_of((1 - pair) * 2560 + d * PIECE, PIECE)
        pltpu.make_async_copy(
            oth.at[d, pl.ds(2 * PIECE, PIECE)],
            dst.at[pl.ds(row, PIECE)],
            sems.at[2 * (1 - pair) + d // 16],
        ).start()


def wait_block(block, sem):
    pltpu.make_async_copy(block, block, sem).wait()


def start_attention_weights(pair, wqkv, wout, oth, w_ref, sems):
    for g in range(4):
        own = wqkv.at[:, pl.ds(g * D, D)] if g < 3 else wout
        start_square(pair, own, oth, 0, w_ref, g * D, sems.at[g], g)


def start_up(pair, wup, oth, w_ref, sems):
    for g in range(4):
        start_square(pair, wup.at[:, pl.ds(g * D, D)], oth, 1, w_ref, g * D, sems.at[g], g)


def attention_forward_kernel(
    ints, x_ref, g1, b1, g2, b2, wqkv, wout, oth,
    qkv_ref, prob_ref, mixed_ref, middle_ref, h1_ref, h2_ref,
    w_ref, sems,
):
    pair = ints[0]
    start_attention_weights(pair, wqkv, wout, oth, w_ref, sems)

    def norm_one(rows):
        hat, _ = stats(x_ref[rows, :].astype(F32))
        h1_ref[rows, :] = (hat * g1[...] + b1[...]).astype(BF)

    row_blocks(ROWS, norm_one)
    for g in range(3):
        wait_block(w_ref.at[:, pl.ds(g * D, D)], sems.at[g])

        def columns(n, carry):
            col = pl.ds(pl.multiple_of(g * D + n * 256, 256), 256)
            qkv_ref[:, col] = dot(h1_ref[...], w_ref[:, col]).astype(BF)
            return carry

        lax.fori_loop(0, 5, columns, 0)
    low = lax.broadcasted_iota(jnp.int32, (SEQ, 128), 1) < 64
    zero = jnp.zeros((SEQ, 128), BF)
    key_at = lax.broadcasted_iota(jnp.int32, (2 * SEQ, SEQ), 1)
    for s in range(2):
        valid = key_at < ints[1 + s]
        rows = pl.ds(s * SEQ, SEQ)

        def heads(i, carry):
            at = pl.multiple_of(i * 128, 128)
            q = qkv_ref[rows, pl.ds(at, 128)] * jnp.asarray(0.125, BF)
            k = qkv_ref[rows, pl.ds(at + D, 128)]
            v = qkv_ref[rows, pl.ds(at + 2 * D, 128)]
            both = jnp.concatenate([jnp.where(low, q, zero), jnp.where(low, zero, q)], axis=0)
            scores = jnp.where(valid, dot(both, k, NT), -1e30)
            raised = jnp.exp(scores - jnp.max(scores, axis=-1, keepdims=True))
            prob = (raised / jnp.sum(raised, axis=-1, keepdims=True)).astype(BF)
            prob_ref[s * 10 + i] = prob
            vv = jnp.concatenate([jnp.where(low, v, zero), jnp.where(low, zero, v)], axis=0)
            side = jnp.concatenate([prob[:SEQ], prob[SEQ:]], axis=1)
            mixed_ref[rows, pl.ds(at, 128)] = dot(side, vv).astype(BF)
            return carry

        lax.fori_loop(0, 10, heads, 0, unroll=2)
    wait_block(w_ref.at[:, pl.ds(3 * D, D)], sems.at[3])

    def out_columns(n, carry):
        col = pl.ds(pl.multiple_of(n * 256, 256), 256)
        wcol = pl.ds(pl.multiple_of(3 * D + n * 256, 256), 256)
        middle_ref[:, col] = x_ref[:, col].astype(F32) + dot(mixed_ref[...], w_ref[:, wcol])
        return carry

    lax.fori_loop(0, 5, out_columns, 0)

    def norm_two(rows):
        hat, _ = stats(middle_ref[rows, :])
        h2_ref[rows, :] = (hat * g2[...] + b2[...]).astype(BF)

    row_blocks(ROWS, norm_two)


def mlp_forward_kernel(
    ints, h2_ref, middle_ref, wup, wdown, oth, y_ref, active_ref, slope_ref, wu_ref, wd_ref, sems
):
    pair = ints[0]
    start_up(pair, wup, oth, wu_ref, sems)
    start_tall(pair, wdown, oth, wd_ref, sems.at[pl.ds(4, 4)])
    for g in range(4):
        wait_block(wu_ref.at[:, pl.ds(g * D, D)], sems.at[g])

        def columns(n, carry):
            col = pl.ds(pl.multiple_of(g * D + n * 256, 256), 256)
            u = dot(h2_ref[...], wu_ref[:, col])
            cdf = 0.5 + 0.5 * lax.erf(u * 0.7071067811865476)
            pdf = 0.3989422804014327 * jnp.exp(-0.5 * u * u)
            active_ref[:, col] = (u * cdf).astype(BF)
            slope_ref[:, col] = (cdf + u * pdf).astype(BF)
            return carry

        lax.fori_loop(0, 5, columns, 0)
    for g in range(4):
        wait_block(wd_ref.at[pl.ds(g * D, D)], sems.at[4 + g])

    def down_columns(n, carry):
        col = pl.ds(pl.multiple_of(n * 256, 256), 256)
        y_ref[:, col] = (middle_ref[:, col] + dot(active_ref[...], wd_ref[:, col])).astype(BF)
        return carry

    lax.fori_loop(0, 5, down_columns, 0)


def fold(total, value):
    for r in range(0, 32, 8):
        total = total + value[r : r + 8]
    return total


def norm_backward(grad_ref, value_of, gain, write, sums_ref):
    nothing = jnp.zeros((8, D), F32)

    def step(i, carry):
        of_gain, of_bias = carry
        rows = pl.ds(pl.multiple_of(i * 32, 32), 32)
        hat, rstd = stats(value_of(rows))
        grad = grad_ref[rows, :]
        scaled = grad * gain[...]
        first = jnp.mean(scaled, axis=-1, keepdims=True)
        second = jnp.mean(scaled * hat, axis=-1, keepdims=True)
        write(rows, rstd * (scaled - first - hat * second))
        return fold(of_gain, grad * hat), fold(of_bias, grad)

    of_gain, of_bias = lax.fori_loop(0, ROWS // 32, step, (nothing, nothing))
    sums_ref[0:1, :] = jnp.sum(of_gain, axis=0, keepdims=True)
    sums_ref[1:2, :] = jnp.sum(of_bias, axis=0, keepdims=True)


def mlp_backward_kernel(
    ints, grad_ref, slope_ref, middle_ref, g2, wup, wdown, oth,
    du_ref, dmiddle_ref, low_ref, sums_ref,
    wu_ref, wd_ref, dh_ref, sems,
):
    pair = ints[0]
    start_tall(pair, wdown, oth, wd_ref, sems.at[pl.ds(4, 4)])
    start_up(pair, wup, oth, wu_ref, sems)
    for g in range(4):
        wait_block(wd_ref.at[pl.ds(g * D, D)], sems.at[4 + g])

        def columns(n, carry):
            col = pl.ds(pl.multiple_of(g * D + n * 256, 256), 256)
            dact = dot(grad_ref[...], wd_ref[col, :], NT)
            du_ref[:, col] = (dact * slope_ref[:, col].astype(F32)).astype(BF)
            return carry

        lax.fori_loop(0, 5, columns, 0)
    for g in range(4):
        wait_block(wu_ref.at[:, pl.ds(g * D, D)], sems.at[g])

    def features(n, carry):
        at = pl.ds(pl.multiple_of(n * 256, 256), 256)
        dh_ref[:, at] = dot(du_ref[...], wu_ref[at, :], NT)
        return carry

    lax.fori_loop(0, 5, features, 0)

    def write(rows, grad):
        total = grad_ref[rows, :].astype(F32) + grad
        dmiddle_ref[rows, :] = total
        low_ref[rows, :] = total.astype(BF)

    norm_backward(dh_ref, lambda rows: middle_ref[rows, :], g2, write, sums_ref)


def attention_backward_kernel(
    ints, low_ref, dmiddle_ref, qkv_ref, prob_ref, x_ref, g1, wqkv, wout, oth,
    dqkv_ref, dx_ref, sums_ref,
    w_ref, dmixed_ref, dh_ref, sems,
):
    pair = ints[0]
    for g in (3, 0, 1, 2):
        own = wqkv.at[:, pl.ds(g * D, D)] if g < 3 else wout
        start_square(pair, own, oth, 0, w_ref, g * D, sems.at[g], g)
    wait_block(w_ref.at[:, pl.ds(3 * D, D)], sems.at[3])

    def out_features(n, carry):
        at = pl.ds(pl.multiple_of(n * 256, 256), 256)
        dmixed_ref[:, at] = dot(low_ref[...], w_ref[at, pl.ds(3 * D, D)], NT).astype(BF)
        return carry

    lax.fori_loop(0, 5, out_features, 0)
    low = lax.broadcasted_iota(jnp.int32, (SEQ, 128), 1) < 64
    zero = jnp.zeros((SEQ, 128), BF)

    def split(v):
        return jnp.concatenate([jnp.where(low, v, zero), jnp.where(low, zero, v)], axis=0)

    for s in range(2):
        rows = pl.ds(s * SEQ, SEQ)

        def heads(i, carry):
            at = pl.multiple_of(i * 128, 128)
            q = qkv_ref[rows, pl.ds(at, 128)] * jnp.asarray(0.125, BF)
            k = qkv_ref[rows, pl.ds(at + D, 128)] * jnp.asarray(0.125, BF)
            v = qkv_ref[rows, pl.ds(at + 2 * D, 128)]
            dm = split(dmixed_ref[rows, pl.ds(at, 128)])
            prob = prob_ref[s * 10 + i]
            dprob = dot(dm, v, NT)
            wide = prob.astype(F32)
            inner = jnp.sum(dprob * wide, axis=-1, keepdims=True)
            dscore = (wide * (dprob - inner)).astype(BF)
            side = jnp.concatenate([dscore[:SEQ], dscore[SEQ:]], axis=1)
            dqkv_ref[rows, pl.ds(at, 128)] = dot(side, split(k)).astype(BF)
            dqkv_ref[rows, pl.ds(at + D, 128)] = dot(dscore, split(q), TN).astype(BF)
            dqkv_ref[rows, pl.ds(at + 2 * D, 128)] = dot(prob, dm, TN).astype(BF)
            return carry

        lax.fori_loop(0, 10, heads, 0, unroll=2)
    for g in range(3):
        wait_block(w_ref.at[:, pl.ds(g * D, D)], sems.at[g])

    def features(n, carry):
        at = pl.ds(pl.multiple_of(n * 256, 256), 256)
        dh_ref[:, at] = dot(dqkv_ref[...], w_ref[at, pl.ds(0, 3 * D)], NT)
        return carry

    lax.fori_loop(0, 5, features, 0)

    def write(rows, grad):
        dx_ref[rows, :] = (dmiddle_ref[rows, :] + grad).astype(BF)

    norm_backward(dh_ref, lambda rows: x_ref[rows, :].astype(F32), g1, write, sums_ref)


def weight_grad_kernel(a_own, a_got, b_own, b_got, first, second):
    half = first.shape[0]
    for at, out in ((0, first), (half, second)):
        rows = pl.ds(at, half)
        out[...] = (
            dot(a_own[rows, :], b_own[...]) + dot(a_got[rows, :], b_got[...])
        ).astype(BF)


VM = pl.BlockSpec(memory_space=pltpu.VMEM)
SM = pl.BlockSpec(memory_space=pltpu.SMEM)
HB = pl.BlockSpec(memory_space=pl.ANY)
LIMIT = 60 * 1024 * 1024


def call(kernel, ins, outs, scratch, specs, flops, moved):
    return pl.pallas_call(
        kernel,
        out_shape=tuple(jax.ShapeDtypeStruct(s, t) for s, t in outs),
        in_specs=specs,
        out_specs=tuple(VM for _ in outs),
        scratch_shapes=scratch,
        compiler_params=pltpu.CompilerParams(vmem_limit_bytes=LIMIT),
        cost_estimate=pl.CostEstimate(flops=flops, bytes_accessed=moved, transcendentals=0),
    )(*ins)


def attention_forward(ints, x, norms, weights):
    g1, b1, g2, b2 = norms
    wqkv, wout, _, _, oth = weights
    return call(
        attention_forward_kernel,
        (ints, x, g1, b1, g2, b2, wqkv, wout, oth),
        [
            ((ROWS, 3 * D), BF), ((20, 2 * SEQ, SEQ), BF), ((ROWS, D), BF),
            ((ROWS, D), F32), ((ROWS, D), BF), ((ROWS, D), BF),
        ],
        [pltpu.VMEM((D, 4 * D), BF), pltpu.SemaphoreType.DMA((4,))],
        [SM, VM, VM, VM, VM, VM, HB, HB, HB],
        2 * ROWS * D * 4 * D, 14 * 2**20,
    )


def mlp_forward(ints, h2, middle, weights):
    _, _, wup, wdown, oth = weights
    return call(
        mlp_forward_kernel,
        (ints, h2, middle, wup, wdown, oth),
        [((ROWS, D), BF), ((ROWS, FF), BF), ((ROWS, FF), BF)],
        [pltpu.VMEM((D, FF), BF), pltpu.VMEM((FF, D), BF), pltpu.SemaphoreType.DMA((8,))],
        [SM, VM, VM, HB, HB, HB],
        4 * ROWS * D * FF, 32 * 2**20,
    )


def mlp_backward(ints, grad, slope, middle, g2, weights):
    _, _, wup, wdown, oth = weights
    return call(
        mlp_backward_kernel,
        (ints, grad, slope, middle, g2, wup, wdown, oth),
        [((ROWS, FF), BF), ((ROWS, D), F32), ((ROWS, D), BF), ((2, D), F32)],
        [
            pltpu.VMEM((D, FF), BF), pltpu.VMEM((FF, D), BF),
            pltpu.VMEM((ROWS, D), F32), pltpu.SemaphoreType.DMA((8,)),
        ],
        [SM, VM, VM, VM, VM, HB, HB, HB],
        4 * ROWS * D * FF, 32 * 2**20,
    )


def attention_backward(ints, low, dmiddle, qkv, prob, x, g1, weights):
    wqkv, wout, _, _, oth = weights
    return call(
        attention_backward_kernel,
        (ints, low, dmiddle, qkv, prob, x, g1, wqkv, wout, oth),
        [((ROWS, 3 * D), BF), ((ROWS, D), BF), ((2, D), F32)],
        [
            pltpu.VMEM((D, 4 * D), BF), pltpu.VMEM((ROWS, D), BF),
            pltpu.VMEM((ROWS, D), F32), pltpu.SemaphoreType.DMA((4,)),
        ],
        [SM, VM, VM, VM, VM, VM, VM, HB, HB, HB],
        2 * ROWS * D * 4 * D, 18 * 2**20,
    )


def weight_grad(a_own, a_got, b_own, b_got, tile):
    rows, k = a_own.shape
    cols = b_own.shape[1]
    whole = pl.BlockSpec((rows, k), lambda j: (0, 0))
    part = pl.BlockSpec((k, tile), lambda j: (0, j))
    out = pl.BlockSpec((rows // 2, tile), lambda j: (0, j))
    return pl.pallas_call(
        weight_grad_kernel,
        grid=(cols // tile,),
        out_shape=(jax.ShapeDtypeStruct((rows // 2, cols), BF),) * 2,
        in_specs=[whole, whole, part, part],
        out_specs=(out, out),
        compiler_params=pltpu.CompilerParams(vmem_limit_bytes=LIMIT),
        cost_estimate=pl.CostEstimate(
            flops=4 * rows * k * cols, bytes_accessed=2 * rows * cols, transcendentals=0
        ),
    )(a_own, a_got, b_own, b_got)


def dp_pairs(move):
    pairs = []
    for z in range(4):
        for y in range(4):
            for c in range(2):
                to = move(z, y, c)
                pairs.append((z * 8 + y * 2 + c, to[0] * 8 + to[1] * 2 + to[2]))
    return pairs


FLIPS = {
    ("y", 1): dp_pairs(lambda z, y, c: (z, y ^ 1, c)),
    ("y", 3): dp_pairs(lambda z, y, c: (z, y ^ 3, c)),
    ("z", 1): dp_pairs(lambda z, y, c: (z ^ 1, y, c)),
    ("z", 3): dp_pairs(lambda z, y, c: (z ^ 3, y, c)),
}
CORE = dp_pairs(lambda z, y, c: (z, y, 1 - c))
SWAP = [(0, 1), (1, 0)]
ORDERS = ((0, 3, 1, 2), (0, 1, 2, 3))


def add_low(a, b):
    return (a.astype(F32) + b.astype(F32)).astype(BF)


def reduce_axis(value, axis, parity, at):
    if parity == 0:
        flips = (1, 3)
        picks = (jnp.where((at == 0) | (at == 3), 0, 1), at // 2)
    else:
        flips = (3, 1)
        picks = (at // 2, at % 2)
    for flip, mine in zip(flips, picks):
        half = value.shape[0] // 2
        send = lax.dynamic_slice_in_dim(value, (1 - mine) * half, half, 0)
        got = lax.ppermute(send, "dp", FLIPS[axis, flip])
        value = add_low(lax.dynamic_slice_in_dim(value, mine * half, half, 0), got)
    return value


def reduce_plane(value, first, parity, at):
    second = "z" if first == "y" else "y"
    value = reduce_axis(value, first, parity, at[first])
    return reduce_axis(value, second, parity, at[second])


def reduce_both(halves, parity, at, pair):
    for_zero = reduce_plane(halves[0], "y", parity, at)
    for_one = reduce_plane(halves[1], "z", parity, at)
    send = jnp.where(pair == 0, for_one, for_zero)
    keep = jnp.where(pair == 0, for_zero, for_one)
    got = lax.ppermute(send, "pair", SWAP)
    return keep.astype(F32) + got.astype(F32)


def reduce_small(value):
    for axis, flip in (("y", 1), ("y", 3), ("z", 1), ("z", 3)):
        value = value + lax.ppermute(value, "dp", FLIPS[axis, flip])
    value = value + lax.ppermute(value, "dp", CORE)
    return value + lax.ppermute(value, "pair", SWAP)


def by_core(a, core):
    count = a.shape[1] // 64
    t = a.T.reshape(2, 4, 4, 2, count, ROWS)
    mine = lax.dynamic_index_in_dim(t, core, 3, keepdims=False)
    send = lax.dynamic_index_in_dim(t, 1 - core, 3, keepdims=False)
    return mine, send


def ordered(t, parity):
    order = ORDERS[parity]
    if parity == 0:
        t = jnp.stack([t[:, i] for i in order], axis=1)
        t = jnp.stack([t[:, :, i] for i in order], axis=2)
    first = jnp.swapaxes(t[0], 0, 1).reshape(-1, ROWS)
    return jnp.concatenate([first, t[1].reshape(-1, ROWS)], axis=0)


def shards(
    tokens, lengths, cotangent, w_qkv, w_out, w_up, w_down,
    norm1_gain, norm1_bias, norm2_gain, norm2_bias,
):
    section = lax.axis_index("section")
    pair = lax.axis_index("pair")
    place = lax.axis_index("dp")
    at = {"z": place // 8, "y": (place // 2) % 4}
    core = place % 2
    ints = jnp.concatenate([pair[None].astype(jnp.int32), lengths[:, 0]])
    norms = (norm1_gain, norm1_bias, norm2_gain, norm2_bias)
    x0 = tokens.reshape(ROWS, D)
    cot = cotangent.reshape(ROWS, D)
    wqkv, wout, wup, wdown = w_qkv[0], w_out[0], w_up[0], w_down[0]

    row = (place % 8) * PIECE
    att_piece = jnp.where(
        at["z"] == 3,
        lax.dynamic_slice(wout, (row, 0), (PIECE, D)),
        lax.dynamic_slice(wqkv, (row, jnp.minimum(at["z"], 2) * D), (PIECE, D)),
    )
    piece = jnp.concatenate(
        [
            att_piece,
            lax.dynamic_slice(wup, (row, at["z"] * D), (PIECE, D)),
            lax.dynamic_slice(wdown, (place * PIECE, 0), (PIECE, D)),
        ],
        axis=0,
    )
    oth = lax.all_gather(lax.ppermute(piece, "pair", SWAP), "dp", axis=0)
    weights = (wqkv, wout, wup, wdown, oth)

    def forward(x):
        qkv, prob, mixed, middle, h1, h2 = attention_forward(ints, x, norms, weights)
        y, active, slope = mlp_forward(ints, h2, middle, weights)
        return y, (x, qkv, prob, mixed, middle, h1, h2, active, slope)

    y, _ = forward(x0)
    arriving = lax.ppermute(y, "section", [(0, 1)])
    y, kept = forward(jnp.where(section == 0, x0, arriving))
    x, qkv, prob, mixed, middle, h1, h2, active, slope = kept

    def backward(grad):
        du, dmiddle, low, sums_two = mlp_backward(ints, grad, slope, middle, norms[2], weights)
        dqkv, dx, sums_one = attention_backward(
            ints, low, dmiddle, qkv, prob, x, norms[0], weights
        )
        return du, low, dqkv, dx, sums_one, sums_two

    arriving = lax.ppermute(backward(cot)[3], "section", [(1, 0)])

    features = [by_core(a, core) for a in (h1, mixed, h2, active)]
    lines = [m.size // ROWS for m, _ in features]
    got = lax.ppermute(
        jnp.concatenate([s.reshape(-1, ROWS) for _, s in features], axis=0), "dp", CORE
    )
    shared = []
    start = 0
    for (mine, _), count in zip(features, lines):
        shared.append((mine, got[start : start + count].reshape(mine.shape)))
        start += count
    rows_of = lambda which, parity: [ordered(t, parity) for t in shared[which]]
    h1_first, h1_second = rows_of(0, 0), rows_of(0, 1)
    mixed_rows, h2_rows, active_rows = rows_of(1, 1), rows_of(2, 0), rows_of(3, 1)

    grad = jnp.where(section == 0, arriving, cot)
    du, low, dqkv, dx, sums_one, sums_two = backward(grad)
    swap = lambda v: lax.ppermute(v, "dp", CORE)
    d_down = weight_grad(*active_rows, grad, swap(grad), 640)
    d_up = weight_grad(*h2_rows, du, swap(du), 1280)
    dqkv_got, low_got = swap(dqkv), swap(low)
    d_qk = weight_grad(*h1_first, dqkv[:, : 2 * D], dqkv_got[:, : 2 * D], 1280)
    d_v = weight_grad(*h1_second, dqkv[:, 2 * D :], dqkv_got[:, 2 * D :], 1280)
    d_out = weight_grad(*mixed_rows, low, low_got, 1280)
    d_vo = [jnp.concatenate([a, b], axis=1) for a, b in zip(d_v, d_out)]

    g_up = reduce_both(d_up, 0, at, pair)
    g_down = reduce_both(d_down, 1, at, pair)
    g_qk = reduce_both(d_qk, 0, at, pair)
    g_vo = reduce_both(d_vo, 1, at, pair)
    sums = reduce_small(jnp.concatenate([sums_one, sums_two], axis=0))
    sums = lax.dynamic_slice(sums, (0, (pair * 32 + place) * 20), (4, 20))
    return (
        y.reshape(1, 2, 1, SEQ, D),
        dx.reshape(1, 2, 1, SEQ, D),
        jnp.concatenate([g_qk, g_vo[:, :D]], axis=1)[None],
        g_vo[:, D:][None],
        g_up[None],
        g_down[None],
        sums[0:1],
        sums[1:2],
        sums[2:3],
        sums[3:4],
    )


def solution(mesh):
    rows = ("pair", "dp")
    in_specs = (
        P(None, rows, None, None),
        P(None, rows),
        P(None, rows, None, None),
        P("section", "pair", None),
        P("section", "pair", None),
        P("section", "pair", None),
        P("section", "pair", None),
        P("section", None),
        P("section", None),
        P("section", None),
        P("section", None),
    )
    out_specs = (
        P("section", None, rows, None, None),
        P("section", None, rows, None, None),
        P("section", rows, None),
        P("section", rows, None),
        P("section", rows, None),
        P("section", rows, None),
        P("section", rows),
        P("section", rows),
        P("section", rows),
        P("section", rows),
    )
    return jax.shard_map(shards, mesh=mesh, in_specs=in_specs, out_specs=out_specs, check_vma=False)
```

```python
import jax
import jax.numpy as jnp
import numpy as np
from jax import lax
from jax.experimental import pallas as pl
from jax.experimental.pallas import tpu as pltpu
from jax.sharding import PartitionSpec as P

D = 1280
FF = 5120
SEQ = 128
ROWS = 2 * SEQ
EPSILON = 1e-05
BF = jnp.bfloat16
F32 = jnp.float32
PIECE = 80

NN = (((1,), (0,)), ((), ()))
NT = (((1,), (1,)), ((), ()))
TN = (((0,), (0,)), ((), ()))


def dot(a, b, dims=NN):
    return lax.dot_general(a, b, dims, preferred_element_type=F32)


def row_blocks(count, body):
    def step(i, carry):
        body(pl.ds(pl.multiple_of(i * 32, 32), 32))
        return carry

    lax.fori_loop(0, count // 32, step, 0, unroll=4)


def tiles(body):
    def step(i, carry):
        body(pl.ds(pl.multiple_of(i * 256, 256), 256))
        return carry

    lax.fori_loop(0, D // 256, step, 0)


def stats(v):
    mean = jnp.mean(v, axis=-1, keepdims=True)
    centred = v - mean
    rstd = lax.rsqrt(jnp.mean(centred * centred, axis=-1, keepdims=True) + EPSILON)
    return centred * rstd, rstd


AHEAD = 3


class Stream:
    def __init__(self):
        self.blocks = []
        self.started = 0

    def add(self, name, copies, target, sem):
        self.blocks.append((name, copies, target, sem))

    def begin(self, upto=AHEAD):
        while self.started < min(upto, len(self.blocks)):
            for copy in self.blocks[self.started][1]():
                copy.start()
            self.started += 1

    def need(self, name):
        at = [block[0] for block in self.blocks].index(name)
        self.begin(at + 1 + AHEAD)
        _, _, target, sem = self.blocks[at]
        pltpu.make_async_copy(target, target, sem).wait()


def square(pair, own, oth, which, dst, col, sem, group):
    def copies():
        yield pltpu.make_async_copy(
            own, dst.at[pl.ds(pl.multiple_of(pair * 640, 640), 640), pl.ds(col, D)], sem
        )
        for r in range(8):
            row = pl.multiple_of((1 - pair) * 640 + r * PIECE, PIECE)
            yield pltpu.make_async_copy(
                oth.at[group * 8 + r, pl.ds(which * PIECE, PIECE)],
                dst.at[pl.ds(row, PIECE), pl.ds(col, D)],
                sem,
            )

    return copies


def add_attention(stream, pair, wqkv, wout, oth, dst, sems, order):
    for g in order:
        own = wqkv.at[:, pl.ds(g * D, D)] if g < 3 else wout
        copies = square(pair, own, oth, 0, dst, g * D, sems.at[g], g)
        stream.add(("att", g), copies, dst.at[:, pl.ds(g * D, D)], sems.at[g])


def add_up(stream, pair, wup, oth, dst, sems):
    for g in range(4):
        copies = square(pair, wup.at[:, pl.ds(g * D, D)], oth, 1, dst, g * D, sems.at[4 + g], g)
        stream.add(("up", g), copies, dst.at[:, pl.ds(g * D, D)], sems.at[4 + g])


def add_down(stream, pair, wdown, oth, dst, sems):
    for g in range(4):

        def copies(g=g):
            yield pltpu.make_async_copy(
                wdown.at[pl.ds(g * 640, 640)],
                dst.at[pl.ds(pl.multiple_of(pair * 2560 + g * 640, 640), 640)],
                sems.at[8 + g],
            )
            for d in range(g * 8, g * 8 + 8):
                row = pl.multiple_of((1 - pair) * 2560 + d * PIECE, PIECE)
                yield pltpu.make_async_copy(
                    oth.at[d, pl.ds(2 * PIECE, PIECE)], dst.at[pl.ds(row, PIECE)], sems.at[8 + g]
                )

        stream.add(("down", g), copies, dst.at[pl.ds(0, D)], sems.at[8 + g])


def forward_attention(ints, x_ref, norms, w_ref, need, qkv_ref, prob_ref, mixed_ref, middle_ref, h1_ref, h2_ref, done):
    g1, b1, g2, b2 = norms

    def norm_one(rows):
        hat, _ = stats(x_ref[rows, :].astype(F32))
        h1_ref[rows, :] = (hat * g1[...] + b1[...]).astype(BF)

    row_blocks(ROWS, norm_one)
    done("h1")
    for g in range(3):
        need(("att", g))
        for n in range(g * D, g * D + D, 256):
            qkv_ref[:, n : n + 256] = dot(h1_ref[...], w_ref[:, n : n + 256]).astype(BF)
    done("qkv")
    low = lax.broadcasted_iota(jnp.int32, (SEQ, 128), 1) < 64
    zero = jnp.zeros((SEQ, 128), BF)
    key_at = lax.broadcasted_iota(jnp.int32, (2 * SEQ, SEQ), 1)

    def split(v):
        return jnp.concatenate([jnp.where(low, v, zero), jnp.where(low, zero, v)], axis=0)

    for s in range(2):
        valid = key_at < ints[1 + s]
        rows = pl.ds(s * SEQ, SEQ)

        def heads(i, carry):
            at = pl.multiple_of(i * 128, 128)
            q = qkv_ref[rows, pl.ds(at, 128)] * jnp.asarray(0.125, BF)
            k = qkv_ref[rows, pl.ds(at + D, 128)]
            v = qkv_ref[rows, pl.ds(at + 2 * D, 128)]
            scores = jnp.where(valid, dot(split(q), k, NT), -1e30)
            raised = jnp.exp(scores - jnp.max(scores, axis=-1, keepdims=True))
            prob = (raised / jnp.sum(raised, axis=-1, keepdims=True)).astype(BF)
            if prob_ref is not None:
                prob_ref[s * 10 + i] = prob
            side = jnp.concatenate([prob[:SEQ], prob[SEQ:]], axis=1)
            mixed_ref[rows, pl.ds(at, 128)] = dot(side, split(v)).astype(BF)
            return carry

        lax.fori_loop(0, 10, heads, 0, unroll=10)
    done("prob")
    done("mixed")
    need(("att", 3))
    for n in range(0, D, 256):
        middle_ref[:, n : n + 256] = x_ref[:, n : n + 256].astype(F32) + dot(
            mixed_ref[...], w_ref[:, 3 * D + n : 3 * D + n + 256]
        )
    done("middle")

    def norm_two(rows):
        hat, _ = stats(middle_ref[rows, :])
        h2_ref[rows, :] = (hat * g2[...] + b2[...]).astype(BF)

    row_blocks(ROWS, norm_two)
    done("h2")


def forward_mlp(h2_ref, middle_ref, wu_ref, wd_ref, need, y_ref, active_ref, slope_ref, done):
    for g in range(4):
        need(("up", g))
        for n in range(g * D, g * D + D, 256):
            u = dot(h2_ref[...], wu_ref[:, n : n + 256])
            cdf = 0.5 + 0.5 * lax.erf(u * 0.7071067811865476)
            active_ref[:, n : n + 256] = (u * cdf).astype(BF)
            if slope_ref is not None:
                pdf = 0.3989422804014327 * jnp.exp(-0.5 * u * u)
                slope_ref[:, n : n + 256] = (cdf + u * pdf).astype(BF)
    done("active")
    done("slope")
    for g in range(4):
        need(("down", g))

    def columns(at):
        y_ref[:, at] = (middle_ref[:, at] + dot(active_ref[...], wd_ref[:, at])).astype(BF)

    tiles(columns)


def nothing_done(name):
    pass


def attention_forward_kernel(
    ints, x_ref, g1, b1, g2, b2, wqkv, wout, oth, middle_ref, h2_ref,
    w_ref, qkv_ref, mixed_ref, h1_ref, sems,
):
    stream = Stream()
    add_attention(stream, ints[0], wqkv, wout, oth, w_ref, sems, range(4))
    stream.begin()
    forward_attention(
        ints, x_ref, (g1, b1, g2, b2), w_ref, stream.need,
        qkv_ref, None, mixed_ref, middle_ref, h1_ref, h2_ref, nothing_done,
    )


def mlp_forward_kernel(
    ints, h2_ref, middle_ref, wup, wdown, oth, y_ref, wu_ref, wd_ref, active_ref, sems
):
    stream = Stream()
    add_up(stream, ints[0], wup, oth, wu_ref, sems)
    add_down(stream, ints[0], wdown, oth, wd_ref, sems)
    stream.begin()
    forward_mlp(
        h2_ref, middle_ref, wu_ref, wd_ref, stream.need, y_ref, active_ref, None, nothing_done
    )


def fold(total, value):
    for r in range(0, 32, 8):
        total = total + value[r : r + 8]
    return total


def norm_backward(grad_ref, value_of, gain, write, sums_ref):
    nothing = jnp.zeros((8, D), F32)

    def step(i, carry):
        of_gain, of_bias = carry
        rows = pl.ds(pl.multiple_of(i * 32, 32), 32)
        hat, rstd = stats(value_of(rows))
        grad = grad_ref[rows, :]
        scaled = grad * gain[...]
        first = jnp.mean(scaled, axis=-1, keepdims=True)
        second = jnp.mean(scaled * hat, axis=-1, keepdims=True)
        write(rows, rstd * (scaled - first - hat * second))
        return fold(of_gain, grad * hat), fold(of_bias, grad)

    of_gain, of_bias = lax.fori_loop(0, ROWS // 32, step, (nothing, nothing), unroll=4)
    if sums_ref is not None:
        sums_ref[0:1, :] = jnp.sum(of_gain, axis=0, keepdims=True)
        sums_ref[1:2, :] = jnp.sum(of_bias, axis=0, keepdims=True)


def backward_mlp(grad_ref, slope_ref, middle_ref, g2, wu_ref, wd_ref, dh_ref, du_ref, dmiddle_ref, low_ref, sums_ref, before=nothing_done, done=nothing_done):
    for g in range(4):
        before(g)
        for n in (g * 640, g * 640 + 256, g * 640 + 512):
            wide = min(256, g * 640 + 640 - n)
            for m in (n, 2560 + n):
                dact = dot(grad_ref[...], wd_ref[m : m + wide, :], NT)
                du_ref[:, m : m + wide] = (dact * slope_ref[:, m : m + wide].astype(F32)).astype(BF)
        done(g)
    before("up")

    def features(at):
        dh_ref[:, at] = dot(du_ref[...], wu_ref[at, :], NT)

    tiles(features)

    def write(rows, grad):
        total = grad_ref[rows, :].astype(F32) + grad
        dmiddle_ref[rows, :] = total
        low_ref[rows, :] = total.astype(BF)

    before("middle")
    norm_backward(dh_ref, lambda rows: middle_ref[rows, :], g2, write, sums_ref)


def backward_heads(low_ref, qkv_ref, prob_ref, w_ref, dmixed_ref, dq, dk, dv, before=nothing_done):
    before("out")
    for n in range(0, D, 256):
        dmixed_ref[:, n : n + 256] = dot(
            low_ref[...], w_ref[n : n + 256, 3 * D : 4 * D], NT
        ).astype(BF)
    before("heads")
    low = lax.broadcasted_iota(jnp.int32, (SEQ, 128), 1) < 64
    zero = jnp.zeros((SEQ, 128), BF)

    def split(v):
        return jnp.concatenate([jnp.where(low, v, zero), jnp.where(low, zero, v)], axis=0)

    for s in range(2):
        rows = pl.ds(s * SEQ, SEQ)

        def heads(i, carry):
            at = pl.multiple_of(i * 128, 128)
            q = qkv_ref[rows, pl.ds(at, 128)] * jnp.asarray(0.125, BF)
            k = qkv_ref[rows, pl.ds(at + D, 128)] * jnp.asarray(0.125, BF)
            v = qkv_ref[rows, pl.ds(at + 2 * D, 128)]
            dm = split(dmixed_ref[rows, pl.ds(at, 128)])
            prob = prob_ref[s * 10 + i]
            dprob = dot(dm, v, NT)
            wide = prob.astype(F32)
            inner = jnp.sum(dprob * wide, axis=-1, keepdims=True)
            dscore = (wide * (dprob - inner)).astype(BF)
            side = jnp.concatenate([dscore[:SEQ], dscore[SEQ:]], axis=1)
            dq[rows, pl.ds(at, 128)] = dot(side, split(k)).astype(BF)
            dk[rows, pl.ds(at, 128)] = dot(dscore, split(q), TN).astype(BF)
            dv[rows, pl.ds(at, 128)] = dot(prob, dm, TN).astype(BF)
            return carry

        lax.fori_loop(0, 10, heads, 0, unroll=10)


def backward_norm_one(dmiddle_ref, dqkv, x_ref, g1, w_ref, dh_ref, dx_ref, sums_ref, before=nothing_done):
    before("qkv")

    def features(at):
        dh_ref[:, at] = dot(dqkv[...], w_ref[at, 0 : 3 * D], NT)

    tiles(features)

    def write(rows, grad):
        dx_ref[rows, :] = (dmiddle_ref[rows, :] + grad).astype(BF)

    before("norm")
    norm_backward(dh_ref, lambda rows: x_ref[rows, :].astype(F32), g1, write, sums_ref)


KEPT = ("x", "h1", "qkv", "prob", "mixed", "middle", "h2", "active", "slope")


def both_ways_kernel(
    ints, x0, arriving, grad_ref, g1, b1, g2, b2, wqkv, wout, wup, wdown, oth,
    y_ref, dx_ref, x_out, h1_out, qkv_out, prob_out, mixed_out, middle_out, h2_out, active_out, slope_out,
    w_ref, wu_ref, wd_ref, x_ref, h1_ref, qkv_ref, prob_ref, mixed_ref, middle_ref, h2_ref,
    active_ref, slope_ref, dh_ref, sems, kept_sems,
):
    stream = Stream()
    add_attention(stream, ints[0], wqkv, wout, oth, w_ref, sems, range(4))
    add_up(stream, ints[0], wup, oth, wu_ref, sems)
    add_down(stream, ints[0], wdown, oth, wd_ref, sems)
    stream.begin()
    refs = dict(zip(KEPT, (x_ref, h1_ref, qkv_ref, prob_ref, mixed_ref, middle_ref, h2_ref, active_ref, slope_ref)))
    outs = dict(zip(KEPT, (x_out, h1_out, qkv_out, prob_out, mixed_out, middle_out, h2_out, active_out, slope_out)))

    def copy(name):
        return pltpu.make_async_copy(refs[name], outs[name], kept_sems.at[KEPT.index(name)])

    def done(name):
        copy(name).start()

    @pl.when(ints[3] == 0)
    def _():
        x_ref[...] = x0[...]

    @pl.when(ints[3] != 0)
    def _():
        x_ref[...] = arriving[...]

    done("x")
    forward_attention(
        ints, x_ref, (g1, b1, g2, b2), w_ref, stream.need,
        qkv_ref, prob_ref, mixed_ref, middle_ref, h1_ref, h2_ref, done,
    )
    forward_mlp(
        h2_ref, middle_ref, wu_ref, wd_ref, stream.need, y_ref, active_ref, slope_ref, done
    )
    for name in ("h1", "qkv", "mixed", "middle", "h2", "active"):
        copy(name).wait()
    backward_mlp(
        grad_ref, slope_ref, middle_ref, g2, wu_ref, wd_ref, dh_ref, active_ref, middle_ref, h1_ref,
        None,
    )
    backward_heads(
        h1_ref, qkv_ref, prob_ref, w_ref, h2_ref,
        qkv_ref.at[:, pl.ds(0, D)], qkv_ref.at[:, pl.ds(D, D)], qkv_ref.at[:, pl.ds(2 * D, D)],
    )
    backward_norm_one(
        middle_ref, qkv_ref, x_ref, g1, w_ref, dh_ref, dx_ref, None
    )
    for name in ("x", "prob", "slope"):
        copy(name).wait()


def mlp_backward_kernel(
    ints, arriving, cot, g2, slope, middle, wup, wdown, oth, du_out, dmiddle_ref, low_ref, sums_ref,
    wu_ref, wd_ref, grad_ref, dh_ref, slope_ref, middle_ref, du_ref, sems, kept_sems,
):
    def halves(g, source, target, sem):
        for h in range(2):
            cols = pl.ds(h * 2560 + g * 640, 640)
            yield pltpu.make_async_copy(source.at[:, cols], target.at[:, cols], sem.at[h])

    get_middle = pltpu.make_async_copy(middle, middle_ref, kept_sems.at[16])
    stream = Stream()
    add_down(stream, ints[0], wdown, oth, wd_ref, sems)
    add_up(stream, ints[0], wup, oth, wu_ref, sems)

    def get_slope(g):
        return halves(g, slope, slope_ref, kept_sems.at[pl.ds(2 * g, 2)])

    def put_du(g):
        return halves(g, du_ref, du_out, kept_sems.at[pl.ds(8 + 2 * g, 2)])

    for g in range(4):
        for copy in get_slope(g):
            copy.start()
        if g < AHEAD:
            stream.begin(g + 1)
    get_middle.start()

    @pl.when(ints[3] == 0)
    def _():
        grad_ref[...] = arriving[...]

    @pl.when(ints[3] != 0)
    def _():
        grad_ref[...] = cot[...]


    def before(step):
        if step == "middle":
            get_middle.wait()
        elif step == "up":
            for g in range(4):
                stream.need(("up", g))
        else:
            for copy in get_slope(step):
                copy.wait()
            stream.need(("down", step))

    def done(g):
        for copy in put_du(g):
            copy.start()

    backward_mlp(
        grad_ref, slope_ref, middle_ref, g2, wu_ref, wd_ref, dh_ref, du_ref, dmiddle_ref, low_ref,
        sums_ref, before, done,
    )
    for g in range(4):
        for copy in put_du(g):
            copy.wait()


def heads_backward_kernel(
    ints, low_ref, qkv, prob, wout, oth, joint_ref,
    w_ref, dmixed_ref, qkv_ref, prob_ref, sems, kept_sems,
):
    stream = Stream()
    add_attention(stream, ints[0], None, wout, oth, w_ref, sems, (3,))
    stream.begin()
    kept = [
        pltpu.make_async_copy(src, dst, kept_sems.at[i])
        for i, (src, dst) in enumerate(((qkv, qkv_ref), (prob, prob_ref)))
    ]
    for copy in kept:
        copy.start()

    def before(name):
        if name == "out":
            stream.need(("att", 3))
        else:
            for copy in kept:
                copy.wait()

    joint_ref[:, 3 * D :] = low_ref[...]
    backward_heads(
        low_ref, qkv_ref, prob_ref, w_ref, dmixed_ref,
        *(joint_ref.at[:, pl.ds(i * D, D)] for i in range(3)), before,
    )


def norm_one_backward_kernel(
    ints, g1, joint_ref, dmiddle, x, wqkv, oth, dx_ref, sums_ref,
    w_ref, dh_ref, dmiddle_ref, x_ref, sems, kept_sems,
):
    stream = Stream()
    add_attention(stream, ints[0], wqkv, None, oth, w_ref, sems, range(3))
    stream.begin()
    kept = [
        pltpu.make_async_copy(src, dst, kept_sems.at[i])
        for i, (src, dst) in enumerate(((dmiddle, dmiddle_ref), (x, x_ref)))
    ]
    for copy in kept:
        copy.start()

    def before(name):
        if name == "qkv":
            for g in range(3):
                stream.need(("att", g))
        else:
            for copy in kept:
                copy.wait()

    backward_norm_one(
        dmiddle_ref, joint_ref.at[:, pl.ds(0, 3 * D)], x_ref, g1, w_ref, dh_ref,
        dx_ref, sums_ref, before,
    )


H1A, H1B, MIXB, H2A, ACT, LINES = 0, 640, 1408, 2176, 2816, 5376


def one_hot(index_ref):
    rows = index_ref.shape[0]
    return jnp.where(
        lax.broadcasted_iota(jnp.int32, (rows, D), 1) == index_ref[...], 1.0, 0.0
    ).astype(BF)


def lay_out_kernel(h1, mixed, h2, active, index_a, index_b, index_c, mine, send, pick):
    def put(value, at, count):
        mine[at : at + count, :] = value[:count].astype(BF)
        send[at : at + count, :] = value[count:].astype(BF)

    pick[0:D, :] = one_hot(index_a)
    put(dot(pick[0:D, :], h1[...], NT), H1A, 640)
    put(dot(pick[0:D, :], h2[...], NT), H2A, 640)
    pick[...] = one_hot(index_b)
    put(dot(pick[...], h1[...], NT), H1B, 768)
    put(dot(pick[...], mixed[...], NT), MIXB, 768)
    pick[0:D, :] = one_hot(index_c)
    for q in range(4):
        value = dot(pick[0:D, :], active[:, q * D : q * D + D], NT).astype(BF)
        for block in range(8):
            z, y = 2 * (q % 2) + block // 4, block % 4
            at = ACT + (y * 4 + z) * 80 if q < 2 else ACT + 1280 + (z * 4 + y) * 80
            mine[at : at + 80, :] = value[block * 80 : block * 80 + 80]
            send[at : at + 80, :] = value[640 + block * 80 : 720 + block * 80]


def parts_of(groups, half):
    group = half // 2
    starts = []
    for p in range(2):
        sent = groups[p]
        starts.append(pl.multiple_of(p * half + sent * group, 16))
        starts.append(pl.multiple_of(p * half + (1 - sent) * group, 16))
    return starts


def rows_product(own, got, starts, group, b_own, b_got, outs, extra=None):
    width = b_own.shape[1]
    for n in range(0, width, 256):
        cols = slice(n, min(n + 256, width))

        def both(left, right):
            return dot(
                jnp.concatenate([left, right], axis=1),
                jnp.concatenate([b_own[:, cols], b_got[:, cols]], axis=0),
            )

        if group <= 200:
            left = jnp.concatenate([own[pl.ds(at, group), :] for at in starts], axis=0)
            right = jnp.concatenate([got[pl.ds(at, group), :] for at in starts], axis=0)
            value = both(left, right)
            if extra is not None and n == 0:
                value = value + jnp.concatenate([extra[pl.ds(at, group), :] for at in starts], axis=0)
            for i, out in enumerate(outs):
                out[:, cols] = value[i * group : i * group + group].astype(BF)
        else:
            for at, out in zip(starts, outs):
                out[:, cols] = both(own[pl.ds(at, group), :], got[pl.ds(at, group), :]).astype(BF)


def load_lines(mine, got, base, own_ref, got_ref, sems):
    count = own_ref.shape[0]
    copies = (
        pltpu.make_async_copy(mine.at[pl.ds(base, count)], own_ref, sems.at[0]),
        pltpu.make_async_copy(got.at[pl.ds(base, count)], got_ref, sems.at[1]),
    )
    for c in copies:
        c.start()
    for c in copies:
        c.wait()


def weight_grad_kernel(base, groups, mine, got, b_own, b_got, *rest):
    outs, (own_ref, got_ref, sems) = rest[:4], rest[4:]

    @pl.when(pl.program_id(0) == 0)
    def _():
        load_lines(mine, got, base, own_ref, got_ref, sems)

    half = own_ref.shape[0] // 2
    rows_product(
        own_ref, got_ref, parts_of(groups, half), half // 2, b_own, b_got, outs
    )


def down_grad_kernel(ints, groups, mine, got, own_a, own_b, got_a, got_b, *rest):
    outs, (own_ref, got_ref, b_own, b_got, sems) = rest[:4], rest[4:]

    @pl.when(pl.program_id(0) == 0)
    def _():
        load_lines(mine, got, ACT, own_ref, got_ref, sems)

    @pl.when(ints[3] == 0)
    def _():
        b_own[...] = own_a[...]
        b_got[...] = got_a[...]

    @pl.when(ints[3] != 0)
    def _():
        b_own[...] = own_b[...]
        b_got[...] = got_b[...]

    half = own_ref.shape[0] // 2
    rows_product(
        own_ref, got_ref, parts_of(groups, half), half // 2, b_own, b_got, outs
    )


def value_out_grad_kernel(groups, mine, got, dv_own, dv_got, low_own, low_got, extra, *rest):
    outs, (own_ref, got_ref, sems) = rest[:4], rest[4:]
    half = own_ref.shape[0] // 2
    starts = parts_of(groups, half)

    @pl.when(pl.program_id(0) == 0)
    def _():
        load_lines(mine, got, H1B, own_ref, got_ref, sems)
        rows_product(
            own_ref, got_ref, starts, half // 2, dv_own, dv_got, outs, extra
        )

    @pl.when(pl.program_id(0) == 1)
    def _():
        load_lines(mine, got, MIXB, own_ref, got_ref, sems)
        rows_product(
            own_ref, got_ref, starts, half // 2, low_own, low_got, outs
        )


VM = pl.BlockSpec(memory_space=pltpu.VMEM)
SM = pl.BlockSpec(memory_space=pltpu.SMEM)
HB = pl.BlockSpec(memory_space=pltpu.HBM)
LIMIT = 60 * 1024 * 1024


def call(kernel, ins, specs, outs, scratch, flops, moved):
    return pl.pallas_call(
        kernel,
        out_shape=tuple(
            (pltpu.HBM if o[2] is HB else jax.ShapeDtypeStruct)(*o[:2]) if isinstance(o, tuple) else o
            for o in outs
        ),
        in_specs=specs,
        out_specs=tuple(o[2] if isinstance(o, tuple) else VM for o in outs),
        scratch_shapes=scratch,
        compiler_params=pltpu.CompilerParams(vmem_limit_bytes=LIMIT),
        cost_estimate=pl.CostEstimate(flops=flops, bytes_accessed=moved, transcendentals=0),
    )(*ins)


def dma(n):
    return pltpu.SemaphoreType.DMA((n,))


TOKENS = ((ROWS, D), BF)
WIDE = ((ROWS, D), F32)
QKV = ((ROWS, 3 * D), BF)
PROB = ((20, 2 * SEQ, SEQ), BF)
HIDDEN = ((ROWS, FF), BF)
SUMS = ((2, D), F32)
ATT_W = pltpu.VMEM((D, 4 * D), BF)
UP_W = pltpu.VMEM((D, FF), BF)
DOWN_W = pltpu.VMEM((FF, D), BF)


def vmem(kind):
    return pltpu.VMEM(*kind)


def attention_forward(ints, x, norms, weights):
    wqkv, wout, _, _, oth = weights
    return call(
        attention_forward_kernel,
        (ints, x, *norms, wqkv, wout, oth),
        [SM, VM, VM, VM, VM, VM, HB, HB, HB],
        [WIDE + (VM,), TOKENS + (VM,)],
        [ATT_W, vmem(QKV), vmem(TOKENS), vmem(TOKENS), dma(4)],
        2 * ROWS * D * 4 * D, 14 * 2**20,
    )


def mlp_forward(ints, h2, middle, weights):
    _, _, wup, wdown, oth = weights
    return call(
        mlp_forward_kernel,
        (ints, h2, middle, wup, wdown, oth),
        [SM, VM, VM, HB, HB, HB],
        [TOKENS + (VM,)],
        [UP_W, DOWN_W, vmem(HIDDEN), dma(12)],
        4 * ROWS * D * FF, 32 * 2**20,
    )[0]


def both_ways(ints, x0, arriving, grad, norms, weights):
    kinds = (TOKENS, TOKENS, QKV, PROB, TOKENS, WIDE, TOKENS, HIDDEN, HIDDEN)
    return call(
        both_ways_kernel,
        (ints, x0, arriving, grad, *norms, *weights),
        [SM] + [VM] * 7 + [HB] * 5,
        [TOKENS + (VM,), TOKENS + (VM,)] + [k + (HB,) for k in kinds],
        [ATT_W, UP_W, DOWN_W] + [vmem(k) for k in kinds] + [vmem(WIDE), dma(12), dma(9)],
        12 * ROWS * D * FF, 60 * 2**20,
    )


def mlp_backward(ints, arriving, cot, slope, middle, g2, weights):
    _, _, wup, wdown, oth = weights
    return call(
        mlp_backward_kernel,
        (ints, arriving, cot, g2, slope, middle, wup, wdown, oth),
        [SM, VM, VM, VM, HB, HB, HB, HB, HB],
        [HIDDEN + (HB,), WIDE + (VM,), TOKENS + (VM,), SUMS + (VM,)],
        [
            UP_W, DOWN_W, vmem(TOKENS), vmem(WIDE), vmem(HIDDEN), vmem(WIDE), vmem(HIDDEN),
            dma(12), dma(17),
        ],
        2**20, 2**16,
    )


def heads_backward(ints, low, qkv, prob, weights):
    _, wout, _, _, oth = weights
    return call(
        heads_backward_kernel,
        (ints, low, qkv, prob, wout, oth),
        [SM, VM] + [HB] * 4,
        [HIDDEN + (VM,)],
        [ATT_W, vmem(TOKENS), vmem(QKV), vmem(PROB), dma(4), dma(2)],
        2**20, 2**16,
    )[0]


def norm_one_backward(ints, g1, joint, dmiddle, x, weights):
    wqkv, _, _, _, oth = weights
    return call(
        norm_one_backward_kernel,
        (ints, g1, joint, dmiddle, x, wqkv, oth),
        [SM, VM, VM] + [HB] * 4,
        [TOKENS + (VM,), SUMS + (VM,)],
        [ATT_W, vmem(WIDE), vmem(WIDE), vmem(TOKENS), dma(4), dma(2)],
        2**20, 2**16,
    )


def lay_out(h1, mixed, h2, active, indices):
    return call(
        lay_out_kernel,
        (h1, mixed, h2, active, *indices),
        [VM] * 7,
        [((LINES, ROWS), BF, VM), ((LINES, ROWS), BF, VM)],
        [pltpu.VMEM((1536, D), BF)],
        2**20, 2**16,
    )


def grad_call(kernel, steps, ins, specs, half, cols, tile, scratch=()):
    group = half // 2
    out = pl.BlockSpec((group, tile), lambda j: (0, j))
    return pl.pallas_call(
        kernel,
        grid=(steps,),
        out_shape=(pltpu.HBM((group, cols), BF),) * 4,
        in_specs=specs,
        out_specs=(out,) * 4,
        scratch_shapes=[
            pltpu.VMEM((2 * half, ROWS), BF), pltpu.VMEM((2 * half, ROWS), BF), *scratch, dma(2)
        ],
        compiler_params=pltpu.CompilerParams(vmem_limit_bytes=LIMIT),
        cost_estimate=pl.CostEstimate(flops=2**20, bytes_accessed=2**16, transcendentals=0),
    )(*ins)


def weight_grad(groups, mine, got, base, half, b_own, b_got, cols, tile):
    part = pl.BlockSpec((ROWS, tile), lambda j: (0, j))
    kernel = lambda *refs: weight_grad_kernel(base, *refs)
    return grad_call(
        kernel, cols // tile, (groups, mine, got, b_own, b_got), [SM, HB, HB, part, part],
        half, cols, tile,
    )


def value_out_grad(groups, mine, got, joint, joint_got, extra):
    value = pl.BlockSpec((ROWS, D), lambda j: (0, 2))
    last = pl.BlockSpec((ROWS, D), lambda j: (0, 3))
    more = pl.BlockSpec((768, 256), lambda j: (0, 0))
    return grad_call(
        value_out_grad_kernel, 2,
        (groups, mine, got, joint, joint_got, joint, joint_got, extra),
        [SM, HB, HB, value, value, last, last, more], 384, 2 * D, D,
    )


def down_grad(ints, groups, mine, got, grads, tile):
    part = pl.BlockSpec((ROWS, tile), lambda j: (0, j))
    return grad_call(
        down_grad_kernel, D // tile, (ints, groups, mine, got, *grads),
        [SM, SM, HB, HB] + [part] * 4, 1280, D, tile,
        (pltpu.VMEM((ROWS, tile), BF), pltpu.VMEM((ROWS, tile), BF)),
    )


def dp_pairs(move):
    pairs = []
    for z in range(4):
        for y in range(4):
            for c in range(2):
                to = move(z, y, c)
                pairs.append((z * 8 + y * 2 + c, to[0] * 8 + to[1] * 2 + to[2]))
    return pairs


FLIPS = {
    ("y", 1): dp_pairs(lambda z, y, c: (z, y ^ 1, c)),
    ("y", 3): dp_pairs(lambda z, y, c: (z, y ^ 3, c)),
    ("z", 1): dp_pairs(lambda z, y, c: (z ^ 1, y, c)),
    ("z", 3): dp_pairs(lambda z, y, c: (z ^ 3, y, c)),
}
CORE = dp_pairs(lambda z, y, c: (z, y, 1 - c))
SWAP = [(0, 1), (1, 0)]
ORDERS = ((0, 3, 1, 2), (0, 1, 2, 3))


def add_low(a, b):
    return (a.astype(F32) + b.astype(F32)).astype(BF)


def layout_rows(spacing, parity, core):
    order = ORDERS[parity]
    rows = []
    for c in (core, 1 - core):
        for p in range(2):
            for first in order:
                for second in order:
                    y, z = (first, second) if p == 0 else (second, first)
                    start = p * 640 + z * 160 + y * 40 + c * 20
                    rows += [start + i if i < 20 else -1 for i in range(spacing)]
    return np.array(rows, np.int32)


def block_rows(core):
    rows = []
    for c in (core, 1 - core):
        for block in range(8):
            rows += [block * 160 + c * 80 + i for i in range(80)]
    return np.array(rows, np.int32)


LAYOUTS = (
    (layout_rows(20, 0, 0), layout_rows(20, 0, 1)),
    (layout_rows(24, 1, 0), layout_rows(24, 1, 1)),
    (block_rows(0), block_rows(1)),
)


def picks_of(parity, at):
    if parity == 0:
        return jnp.where((at == 0) | (at == 3), 0, 1), at // 2
    return at // 2, at % 2


def flips_of(parity):
    return (1, 3) if parity == 0 else (3, 1)


class Flights:
    WINDOW = 5

    def __init__(self):
        self.gots = []

    def send(self, value, axis, flip):
        if len(self.gots) >= self.WINDOW:
            value, _ = lax.optimization_barrier((value, self.gots[-self.WINDOW]))
        got = (
            lax.ppermute(value, "pair", SWAP)
            if axis == "x"
            else lax.ppermute(value, "dp", FLIPS[axis, flip])
        )
        self.gots.append(got)
        return got


class Rings:
    def __init__(self, flights, send, keep, axes, parity, at):
        self.flights, self.to_send, self.keep = flights, send, keep
        self.plan = [
            (axis, flip, pick)
            for axis in axes
            for flip, pick in zip(flips_of(parity), picks_of(parity, at[axis]))
        ]
        self.step = 0

    def start(self):
        axis, flip, _ = self.plan[self.step]
        self.got = self.flights.send(self.to_send, axis, flip)
        self.step += 1

    def finish(self):
        value = add_low(self.keep, self.got)
        if self.step < 4:
            self.split(value)
        return value

    def finish_first(self):
        return add_low(self.keep, self.got)

    def split(self, value):
        pick = self.plan[self.step][2]
        half = value.shape[0] // 2
        self.to_send = lax.dynamic_slice_in_dim(value, (1 - pick) * half, half, 0)
        self.keep = lax.dynamic_slice_in_dim(value, pick * half, half, 0)


def join_up(up, qk):
    return jnp.concatenate([up, qk], axis=1)


def join_down(down, vo):
    return jnp.concatenate(
        [down.reshape(4, 80, D), vo[:, :D].reshape(4, 24, D), vo[:, D:].reshape(4, 24, D)], axis=1
    ).reshape(-1, D)


def over_pair(flights, values, pair):
    send = jnp.where(pair == 0, values[1], values[0])
    keep = jnp.where(pair == 0, values[0], values[1])
    return keep.astype(F32) + flights.send(send, "x", 1).astype(F32)


def sums_rows(sums):
    t = sums.reshape(4, 2, 4, 4, 2, 20)
    first = jnp.transpose(t[:, 0], (2, 1, 3, 0, 4)).reshape(1, 16, 1, 160)
    second = jnp.transpose(t[:, 1], (1, 2, 3, 0, 4)).reshape(1, 16, 1, 160)
    t = jnp.concatenate([first, second], axis=0)
    return jnp.pad(t, ((0, 0), (0, 0), (20, 3), (0, 96))).reshape(768, 256)


def shards(
    tokens, lengths, cotangent, w_qkv, w_out, w_up, w_down,
    norm1_gain, norm1_bias, norm2_gain, norm2_bias,
):
    section = lax.axis_index("section")
    pair = lax.axis_index("pair")
    place = lax.axis_index("dp")
    at = {"z": place // 8, "y": (place // 2) % 4}
    core = place % 2
    swap = lambda v: lax.ppermute(v, "dp", CORE)
    ints = jnp.concatenate(
        [pair[None].astype(jnp.int32), lengths[:, 0], section[None].astype(jnp.int32)]
    )
    groups = [
        jnp.stack([1 - picks_of(k, at["y"])[0], 1 - picks_of(k, at["z"])[0]]).astype(jnp.int32)
        for k in range(2)
    ]
    indices = [jnp.where(core == 0, a, b)[:, None] for a, b in LAYOUTS]
    norms = (norm1_gain, norm1_bias, norm2_gain, norm2_bias)
    x0 = tokens.reshape(ROWS, D)
    cot = cotangent.reshape(ROWS, D)
    cot_got = swap(cot)
    wqkv, wout, wup, wdown = w_qkv[0], w_out[0], w_up[0], w_down[0]

    row = (place % 8) * PIECE
    att_piece = jnp.where(
        at["z"] == 3,
        lax.dynamic_slice(wout, (row, 0), (PIECE, D)),
        lax.dynamic_slice(wqkv, (row, jnp.minimum(at["z"], 2) * D), (PIECE, D)),
    )
    piece = jnp.concatenate(
        [
            att_piece,
            lax.dynamic_slice(wup, (row, at["z"] * D), (PIECE, D)),
            lax.dynamic_slice(wdown, (place * PIECE, 0), (PIECE, D)),
        ],
        axis=0,
    )
    oth = lax.all_gather(lax.ppermute(piece, "pair", SWAP), "dp", axis=0)

    ints, groups, indices, cot_got, oth = lax.optimization_barrier(
        (ints, groups, indices, cot_got, oth)
    )
    weights = (wqkv, wout, wup, wdown, oth)
    middle, h2 = attention_forward(ints, x0, norms, weights)
    y = mlp_forward(ints, h2, middle, weights)
    arriving = lax.ppermute(y, "section", [(0, 1)])
    y, dx, x, h1, qkv, prob, mixed, middle, h2, active, slope = both_ways(
        ints, x0, arriving, cot, norms, weights
    )
    arriving = lax.ppermute(dx, "section", [(1, 0)])

    mine, send = lay_out(h1, mixed, h2, active, indices)
    got = swap(send)
    arriving, got = lax.optimization_barrier((arriving, got))
    grads = (arriving, cot, swap(arriving), cot_got)
    du, dmiddle, low, sums_two = mlp_backward(
        ints, arriving, cot, slope, middle, norm2_gain, weights
    )
    du_got = swap(du)
    joint = heads_backward(ints, low, qkv, prob, weights)
    joint_got = swap(joint)
    joint, du, du_got = lax.optimization_barrier((joint, du, du_got))
    d_up = weight_grad(groups[0], mine, got, H2A, 320, du, du_got, FF, D)
    grads, d_up = lax.optimization_barrier((grads, d_up))
    d_down = down_grad(ints, groups[1], mine, got, grads, 640)
    joint, dmiddle, d_down = lax.optimization_barrier((joint, dmiddle, d_down))
    dx, sums_one = norm_one_backward(ints, norm1_gain, joint, dmiddle, x, weights)
    dx, sums_one, joint, joint_got, place, pair = lax.optimization_barrier(
        (dx, sums_one, joint, joint_got, place, pair)
    )
    at = {"z": place // 8, "y": (place // 2) % 4}
    d_qk = weight_grad(groups[0], mine, got, H1A, 320, joint, joint_got, 2 * D, D)
    extra = sums_rows(jnp.concatenate([sums_one, sums_two], axis=0))
    extra, d_qk = lax.optimization_barrier((extra, d_qk))
    d_vo = value_out_grad(groups[1], mine, got, joint, joint_got, extra)
    keeps = [d[i] for d in (d_up, d_down, d_vo, d_qk) for i in (1, 3)]
    keeps = lax.optimization_barrier(keeps)
    d_up, d_down, d_vo, d_qk = (
        (d[0], keeps[2 * i], d[2], keeps[2 * i + 1])
        for i, d in enumerate((d_up, d_down, d_vo, d_qk))
    )

    flights = Flights()

    def rings(parts, parity):
        return [
            Rings(flights, parts[0], parts[1], "yz", parity, at),
            Rings(flights, parts[2], parts[3], "zy", parity, at),
        ]

    def each(method, group):
        return [getattr(r, method)() for r in group]

    down, up, vo, qk = rings(d_down, 1), rings(d_up, 0), rings(d_vo, 1), rings(d_qk, 0)
    def phase(now, later):
        each("start", now)
        gots, sends = lax.optimization_barrier(
            ([r.got for r in now], [r.to_send for r in later])
        )
        for r, v in zip(now, gots):
            r.got = v
        for r, v in zip(later, sends):
            r.to_send = v

    phase(down + up, vo + qk)
    each("finish", down + up)
    phase(vo + qk, down + up)
    each("finish", vo + qk)
    phase(down + up, vo + qk)
    each("start", vo + qk)
    for one, two, join in ((down, vo, join_down), (up, qk, join_up)):
        for a, b in zip(one, two):
            value = join(a.finish_first(), b.finish_first())
            a.split(value)
    each("start", down + up)
    each("finish", down + up)
    each("start", down + up)
    g_down = over_pair(flights, each("finish", down), pair)
    g_up = over_pair(flights, each("finish", up), pair)
    sums = g_down[100, :160].reshape(2, 80)
    sums = (
        lax.dynamic_index_in_dim(sums, place % 2, 0, keepdims=False)
        + swap(lax.dynamic_index_in_dim(sums, 1 - place % 2, 0, keepdims=False))
    ).reshape(4, 20)
    return (
        y.reshape(1, 2, 1, SEQ, D),
        dx.reshape(1, 2, 1, SEQ, D),
        jnp.concatenate([g_up[:, FF:], g_down[80:100]], axis=1)[None],
        g_down[104:124][None],
        g_up[:, :FF][None],
        g_down[:80][None],
        sums[0:1],
        sums[1:2],
        sums[2:3],
        sums[3:4],
    )


def solution(mesh):
    rows = ("pair", "dp")
    in_specs = (
        P(None, rows, None, None),
        P(None, rows),
        P(None, rows, None, None),
        P("section", "pair", None),
        P("section", "pair", None),
        P("section", "pair", None),
        P("section", "pair", None),
        P("section", None),
        P("section", None),
        P("section", None),
        P("section", None),
    )
    out_specs = (
        P("section", None, rows, None, None),
        P("section", None, rows, None, None),
        P("section", rows, None),
        P("section", rows, None),
        P("section", rows, None),
        P("section", rows, None),
        P("section", rows),
        P("section", rows),
        P("section", rows),
        P("section", rows),
    )
    return jax.shard_map(shards, mesh=mesh, in_specs=in_specs, out_specs=out_specs, check_vma=False)
```

```python
import jax
import jax.numpy as jnp
import numpy as np
from jax import lax
from jax.experimental import pallas as pl
from jax.experimental.pallas import tpu as pltpu
from jax.sharding import PartitionSpec as P

D = 1280
FF = 5120
SEQ = 128
ROWS = 2 * SEQ
EPSILON = 1e-05
BF = jnp.bfloat16
F32 = jnp.float32
PIECE = 80

NN = (((1,), (0,)), ((), ()))
NT = (((1,), (1,)), ((), ()))
TN = (((0,), (0,)), ((), ()))


def dot(a, b, dims=NN):
    return lax.dot_general(a, b, dims, preferred_element_type=F32)


def row_blocks(count, body):
    def step(i, carry):
        body(pl.ds(pl.multiple_of(i * 32, 32), 32))
        return carry

    lax.fori_loop(0, count // 32, step, 0, unroll=4)


def tiles(body):
    def step(i, carry):
        body(pl.ds(pl.multiple_of(i * 256, 256), 256))
        return carry

    lax.fori_loop(0, D // 256, step, 0)


def stats(v):
    mean = jnp.mean(v, axis=-1, keepdims=True)
    centred = v - mean
    rstd = lax.rsqrt(jnp.mean(centred * centred, axis=-1, keepdims=True) + EPSILON)
    return centred * rstd, rstd


AHEAD = 3


class Stream:
    def __init__(self):
        self.blocks = []
        self.started = 0

    def add(self, name, copies, target, sem):
        self.blocks.append((name, copies, target, sem))

    def begin(self, upto=AHEAD):
        while self.started < min(upto, len(self.blocks)):
            for copy in self.blocks[self.started][1]():
                copy.start()
            self.started += 1

    def need(self, name):
        at = [block[0] for block in self.blocks].index(name)
        self.begin(at + 1 + AHEAD)
        _, _, target, sem = self.blocks[at]
        pltpu.make_async_copy(target, target, sem).wait()


def square(pair, own, oth, which, dst, col, sem, group):
    def copies():
        yield pltpu.make_async_copy(
            own, dst.at[pl.ds(pl.multiple_of(pair * 640, 640), 640), pl.ds(col, D)], sem
        )
        for r in range(8):
            row = pl.multiple_of((1 - pair) * 640 + r * PIECE, PIECE)
            yield pltpu.make_async_copy(
                oth.at[group * 8 + r, pl.ds(which * PIECE, PIECE)],
                dst.at[pl.ds(row, PIECE), pl.ds(col, D)],
                sem,
            )

    return copies


def add_attention(stream, pair, wqkv, wout, oth, dst, sems, order):
    for g in order:
        own = wqkv.at[:, pl.ds(g * D, D)] if g < 3 else wout
        copies = square(pair, own, oth, 0, dst, g * D, sems.at[g], g)
        stream.add(("att", g), copies, dst.at[:, pl.ds(g * D, D)], sems.at[g])


def add_up(stream, pair, wup, oth, dst, sems):
    for g in range(4):
        copies = square(pair, wup.at[:, pl.ds(g * D, D)], oth, 1, dst, g * D, sems.at[4 + g], g)
        stream.add(("up", g), copies, dst.at[:, pl.ds(g * D, D)], sems.at[4 + g])


DIRECT, TAIL = 2048, 16
DOWN_BLOCKS = ((True, 0, 1280), (True, 1280, 1280), (False, 0, DIRECT), (False, DIRECT, 512))


def down_row(pair, block, n=0):
    own, start, _ = DOWN_BLOCKS[block]
    return pl.multiple_of((pair if own else 1 - pair) * 2560 + start + n, 256)


def add_down(stream, pair, core, wdown, near, far, oth, dst, sems):
    def own(block):
        _, start, rows = DOWN_BLOCKS[block]
        yield pltpu.make_async_copy(
            wdown.at[pl.ds(start, rows)],
            dst.at[pl.ds(down_row(pair, block), rows)],
            sems.at[8 + block],
        )

    def direct():
        half = DIRECT // 2
        for source, part in ((near, core), (far, 1 - core)):
            row = pl.multiple_of((1 - pair) * 2560 + part * half, half // 2)
            yield pltpu.make_async_copy(source, dst.at[pl.ds(row, half)], sems.at[10])

    def tail():
        for d in range(32):
            row = pl.multiple_of((1 - pair) * 2560 + DIRECT + d * TAIL, TAIL)
            yield pltpu.make_async_copy(
                oth.at[d, pl.ds(2 * PIECE, TAIL)], dst.at[pl.ds(row, TAIL)], sems.at[11]
            )

    plans = (lambda: own(0), lambda: own(1), direct, tail)
    for block, copies in enumerate(plans):
        target = dst.at[pl.ds(0, DOWN_BLOCKS[block][2])]
        stream.add(("down", block), copies, target, sems.at[8 + block])


def forward_attention(ints, x_ref, norms, w_ref, need, qkv_ref, prob_ref, mixed_ref, middle_ref, h1_ref, h2_ref, done):
    g1, b1, g2, b2 = norms

    def norm_one(rows):
        hat, _ = stats(x_ref[rows, :].astype(F32))
        h1_ref[rows, :] = (hat * g1[...] + b1[...]).astype(BF)

    row_blocks(ROWS, norm_one)
    done("h1")
    for g in range(3):
        need(("att", g))
        for n in range(g * D, g * D + D, 256):
            qkv_ref[:, n : n + 256] = dot(h1_ref[...], w_ref[:, n : n + 256]).astype(BF)
    done("qkv")
    low = lax.broadcasted_iota(jnp.int32, (SEQ, 128), 1) < 64
    zero = jnp.zeros((SEQ, 128), BF)
    key_at = lax.broadcasted_iota(jnp.int32, (2 * SEQ, SEQ), 1)

    def split(v):
        return jnp.concatenate([jnp.where(low, v, zero), jnp.where(low, zero, v)], axis=0)

    for s in range(2):
        valid = key_at < ints[1 + s]
        rows = pl.ds(s * SEQ, SEQ)

        def heads(i, carry):
            at = pl.multiple_of(i * 128, 128)
            q = qkv_ref[rows, pl.ds(at, 128)] * jnp.asarray(0.125, BF)
            k = qkv_ref[rows, pl.ds(at + D, 128)]
            v = qkv_ref[rows, pl.ds(at + 2 * D, 128)]
            scores = jnp.where(valid, dot(split(q), k, NT), -1e30)
            raised = jnp.exp(scores - jnp.max(scores, axis=-1, keepdims=True))
            prob = (raised / jnp.sum(raised, axis=-1, keepdims=True)).astype(BF)
            if prob_ref is not None:
                prob_ref[s * 10 + i] = prob
            side = jnp.concatenate([prob[:SEQ], prob[SEQ:]], axis=1)
            mixed_ref[rows, pl.ds(at, 128)] = dot(side, split(v)).astype(BF)
            return carry

        lax.fori_loop(0, 10, heads, 0, unroll=10)
    done("prob")
    done("mixed")
    need(("att", 3))
    for n in range(0, D, 256):
        middle_ref[:, n : n + 256] = x_ref[:, n : n + 256].astype(F32) + dot(
            mixed_ref[...], w_ref[:, 3 * D + n : 3 * D + n + 256]
        )
    done("middle")

    def norm_two(rows):
        hat, _ = stats(middle_ref[rows, :])
        h2_ref[rows, :] = (hat * g2[...] + b2[...]).astype(BF)

    row_blocks(ROWS, norm_two)
    done("h2")


def forward_mlp(h2_ref, middle_ref, wu_ref, wd_ref, need, y_ref, active_ref, slope_ref, done):
    for g in range(4):
        need(("up", g))
        for n in range(g * D, g * D + D, 256):
            u = dot(h2_ref[...], wu_ref[:, n : n + 256])
            cdf = 0.5 + 0.5 * lax.erf(u * 0.7071067811865476)
            active_ref[:, n : n + 256] = (u * cdf).astype(BF)
            if slope_ref is not None:
                pdf = 0.3989422804014327 * jnp.exp(-0.5 * u * u)
                slope_ref[:, n : n + 256] = (cdf + u * pdf).astype(BF)
    done("active")
    done("slope")
    for g in range(4):
        need(("down", g))

    def columns(at):
        y_ref[:, at] = (middle_ref[:, at] + dot(active_ref[...], wd_ref[:, at])).astype(BF)

    tiles(columns)


def nothing_done(name):
    pass


def forward_kernel(
    ints, x_ref, g1, b1, g2, b2, wqkv, wout, wup, wdown, near, far, oth, y_ref,
    w_ref, wu_ref, wd_ref, qkv_ref, mixed_ref, middle_ref, h1_ref, h2_ref, active_ref, sems,
):
    stream = Stream()
    add_attention(stream, ints[0], wqkv, wout, oth, w_ref, sems, range(4))
    add_up(stream, ints[0], wup, oth, wu_ref, sems)
    add_down(stream, ints[0], ints[4], wdown, near, far, oth, wd_ref, sems)
    stream.begin()
    forward_attention(
        ints, x_ref, (g1, b1, g2, b2), w_ref, stream.need,
        qkv_ref, None, mixed_ref, middle_ref, h1_ref, h2_ref, nothing_done,
    )
    forward_mlp(
        h2_ref, middle_ref, wu_ref, wd_ref, stream.need, y_ref, active_ref, None, nothing_done
    )


def fold(total, value):
    for r in range(0, 32, 8):
        total = total + value[r : r + 8]
    return total


def norm_backward(grad_ref, value_of, gain, write, sums_ref):
    nothing = jnp.zeros((8, D), F32)

    def step(i, carry):
        of_gain, of_bias = carry
        rows = pl.ds(pl.multiple_of(i * 32, 32), 32)
        hat, rstd = stats(value_of(rows))
        grad = grad_ref[rows, :]
        scaled = grad * gain[...]
        first = jnp.mean(scaled, axis=-1, keepdims=True)
        second = jnp.mean(scaled * hat, axis=-1, keepdims=True)
        write(rows, rstd * (scaled - first - hat * second))
        return fold(of_gain, grad * hat), fold(of_bias, grad)

    of_gain, of_bias = lax.fori_loop(0, ROWS // 32, step, (nothing, nothing), unroll=4)
    if sums_ref is not None:
        sums_ref[0:1, :] = jnp.sum(of_gain, axis=0, keepdims=True)
        sums_ref[1:2, :] = jnp.sum(of_bias, axis=0, keepdims=True)


def backward_mlp(pair, grad_ref, slope_ref, middle_ref, g2, wu_ref, wd_ref, dh_ref, du_ref, dmiddle_ref, low_ref, sums_ref, before=nothing_done, done=nothing_done):
    for block in range(4):
        before(block)
        for n in range(0, DOWN_BLOCKS[block][2], 256):
            at = pl.ds(down_row(pair, block, n), 256)
            dact = dot(grad_ref[...], wd_ref[at, :], NT)
            du_ref[:, at] = (dact * slope_ref[:, at].astype(F32)).astype(BF)
        done(block)
    before("up")

    def features(at):
        dh_ref[:, at] = dot(du_ref[...], wu_ref[at, :], NT)

    tiles(features)

    def write(rows, grad):
        total = grad_ref[rows, :].astype(F32) + grad
        dmiddle_ref[rows, :] = total
        low_ref[rows, :] = total.astype(BF)

    before("middle")
    norm_backward(dh_ref, lambda rows: middle_ref[rows, :], g2, write, sums_ref)


def backward_heads(low_ref, qkv_ref, prob_ref, w_ref, dmixed_ref, dq, dk, dv, before=nothing_done):
    before("out")
    for n in range(0, D, 256):
        dmixed_ref[:, n : n + 256] = dot(
            low_ref[...], w_ref[n : n + 256, 3 * D : 4 * D], NT
        ).astype(BF)
    before("heads")
    low = lax.broadcasted_iota(jnp.int32, (SEQ, 128), 1) < 64
    zero = jnp.zeros((SEQ, 128), BF)

    def split(v):
        return jnp.concatenate([jnp.where(low, v, zero), jnp.where(low, zero, v)], axis=0)

    for s in range(2):
        rows = pl.ds(s * SEQ, SEQ)

        def heads(i, carry):
            at = pl.multiple_of(i * 128, 128)
            q = qkv_ref[rows, pl.ds(at, 128)] * jnp.asarray(0.125, BF)
            k = qkv_ref[rows, pl.ds(at + D, 128)] * jnp.asarray(0.125, BF)
            v = qkv_ref[rows, pl.ds(at + 2 * D, 128)]
            dm = split(dmixed_ref[rows, pl.ds(at, 128)])
            prob = prob_ref[s * 10 + i]
            dprob = dot(dm, v, NT)
            wide = prob.astype(F32)
            inner = jnp.sum(dprob * wide, axis=-1, keepdims=True)
            dscore = (wide * (dprob - inner)).astype(BF)
            side = jnp.concatenate([dscore[:SEQ], dscore[SEQ:]], axis=1)
            dq[rows, pl.ds(at, 128)] = dot(side, split(k)).astype(BF)
            dk[rows, pl.ds(at, 128)] = dot(dscore, split(q), TN).astype(BF)
            dv[rows, pl.ds(at, 128)] = dot(prob, dm, TN).astype(BF)
            return carry

        lax.fori_loop(0, 10, heads, 0, unroll=10)


def backward_norm_one(dmiddle_ref, dqkv, x_ref, g1, w_ref, dh_ref, dx_ref, sums_ref, before=nothing_done):
    before("qkv")

    def features(at):
        dh_ref[:, at] = dot(dqkv[...], w_ref[at, 0 : 3 * D], NT)

    tiles(features)

    def write(rows, grad):
        dx_ref[rows, :] = (dmiddle_ref[rows, :] + grad).astype(BF)

    before("norm")
    norm_backward(dh_ref, lambda rows: x_ref[rows, :].astype(F32), g1, write, sums_ref)


KEPT = ("x", "h1", "qkv", "prob", "mixed", "middle", "h2", "active", "slope")


def both_ways_kernel(
    ints, x0, arriving, grad_ref, g1, b1, g2, b2, wqkv, wout, wup, wdown, near, far, oth,
    y_ref, dx_ref, x_out, h1_out, qkv_out, prob_out, mixed_out, middle_out, h2_out, active_out, slope_out,
    w_ref, wu_ref, wd_ref, x_ref, h1_ref, qkv_ref, prob_ref, mixed_ref, middle_ref, h2_ref,
    active_ref, slope_ref, dh_ref, sems, kept_sems,
):
    stream = Stream()
    add_attention(stream, ints[0], wqkv, wout, oth, w_ref, sems, range(4))
    add_up(stream, ints[0], wup, oth, wu_ref, sems)
    add_down(stream, ints[0], ints[4], wdown, near, far, oth, wd_ref, sems)
    stream.begin()
    refs = dict(zip(KEPT, (x_ref, h1_ref, qkv_ref, prob_ref, mixed_ref, middle_ref, h2_ref, active_ref, slope_ref)))
    outs = dict(zip(KEPT, (x_out, h1_out, qkv_out, prob_out, mixed_out, middle_out, h2_out, active_out, slope_out)))

    def copy(name):
        return pltpu.make_async_copy(refs[name], outs[name], kept_sems.at[KEPT.index(name)])

    def done(name):
        copy(name).start()

    @pl.when(ints[3] == 0)
    def _():
        x_ref[...] = x0[...]

    @pl.when(ints[3] != 0)
    def _():
        x_ref[...] = arriving[...]

    done("x")
    forward_attention(
        ints, x_ref, (g1, b1, g2, b2), w_ref, stream.need,
        qkv_ref, prob_ref, mixed_ref, middle_ref, h1_ref, h2_ref, done,
    )
    forward_mlp(
        h2_ref, middle_ref, wu_ref, wd_ref, stream.need, y_ref, active_ref, slope_ref, done
    )
    for name in ("h1", "qkv", "mixed", "middle", "h2", "active"):
        copy(name).wait()
    backward_mlp(
        ints[0], grad_ref, slope_ref, middle_ref, g2, wu_ref, wd_ref, dh_ref, active_ref, middle_ref, h1_ref,
        None,
    )
    backward_heads(
        h1_ref, qkv_ref, prob_ref, w_ref, h2_ref,
        qkv_ref.at[:, pl.ds(0, D)], qkv_ref.at[:, pl.ds(D, D)], qkv_ref.at[:, pl.ds(2 * D, D)],
    )
    backward_norm_one(
        middle_ref, qkv_ref, x_ref, g1, w_ref, dh_ref, dx_ref, None
    )
    for name in ("x", "prob", "slope"):
        copy(name).wait()


def mlp_backward_kernel(
    ints, arriving, cot, g2, slope, middle, wup, wdown, near, far, oth, du_out, dmiddle_ref, low_ref, sums_ref,
    wu_ref, wd_ref, grad_ref, dh_ref, slope_ref, middle_ref, du_ref, sems, kept_sems,
):
    def part(block, source, target, sem):
        cols = pl.ds(down_row(ints[0], block), DOWN_BLOCKS[block][2])
        return pltpu.make_async_copy(source.at[:, cols], target.at[:, cols], sem)

    get_middle = pltpu.make_async_copy(middle, middle_ref, kept_sems.at[16])
    stream = Stream()
    add_down(stream, ints[0], ints[4], wdown, near, far, oth, wd_ref, sems)
    add_up(stream, ints[0], wup, oth, wu_ref, sems)

    def get_slope(g):
        return part(g, slope, slope_ref, kept_sems.at[g])

    def put_du(g):
        return part(g, du_ref, du_out, kept_sems.at[8 + g])

    for g in range(4):
        get_slope(g).start()
        if g < AHEAD:
            stream.begin(g + 1)
    get_middle.start()

    @pl.when(ints[3] == 0)
    def _():
        grad_ref[...] = arriving[...]

    @pl.when(ints[3] != 0)
    def _():
        grad_ref[...] = cot[...]


    def before(step):
        if step == "middle":
            get_middle.wait()
        elif step == "up":
            for g in range(4):
                stream.need(("up", g))
        else:
            get_slope(step).wait()
            stream.need(("down", step))

    def done(g):
        put_du(g).start()

    backward_mlp(
        ints[0], grad_ref, slope_ref, middle_ref, g2, wu_ref, wd_ref, dh_ref, du_ref, dmiddle_ref, low_ref,
        sums_ref, before, done,
    )
    for g in range(4):
        put_du(g).wait()


def heads_backward_kernel(
    ints, low_ref, qkv, prob, wout, oth, joint_ref,
    w_ref, dmixed_ref, qkv_ref, prob_ref, sems, kept_sems,
):
    stream = Stream()
    add_attention(stream, ints[0], None, wout, oth, w_ref, sems, (3,))
    stream.begin()
    kept = [
        pltpu.make_async_copy(src, dst, kept_sems.at[i])
        for i, (src, dst) in enumerate(((qkv, qkv_ref), (prob, prob_ref)))
    ]
    for copy in kept:
        copy.start()

    def before(name):
        if name == "out":
            stream.need(("att", 3))
        else:
            for copy in kept:
                copy.wait()

    joint_ref[:, 3 * D :] = low_ref[...]
    backward_heads(
        low_ref, qkv_ref, prob_ref, w_ref, dmixed_ref,
        *(joint_ref.at[:, pl.ds(i * D, D)] for i in range(3)), before,
    )


def norm_one_backward_kernel(
    ints, g1, joint_ref, dmiddle, x, wqkv, oth, dx_ref, sums_ref,
    w_ref, dh_ref, dmiddle_ref, x_ref, sems, kept_sems,
):
    stream = Stream()
    add_attention(stream, ints[0], wqkv, None, oth, w_ref, sems, range(3))
    stream.begin()
    kept = [
        pltpu.make_async_copy(src, dst, kept_sems.at[i])
        for i, (src, dst) in enumerate(((dmiddle, dmiddle_ref), (x, x_ref)))
    ]
    for copy in kept:
        copy.start()

    def before(name):
        if name == "qkv":
            for g in range(3):
                stream.need(("att", g))
        else:
            for copy in kept:
                copy.wait()

    backward_norm_one(
        dmiddle_ref, joint_ref.at[:, pl.ds(0, 3 * D)], x_ref, g1, w_ref, dh_ref,
        dx_ref, sums_ref, before,
    )


H1A, H1B, MIXB, H2A, ACT, LINES = 0, 640, 1408, 2176, 2816, 5376


def one_hot(index_ref):
    rows = index_ref.shape[0]
    return jnp.where(
        lax.broadcasted_iota(jnp.int32, (rows, D), 1) == index_ref[...], 1.0, 0.0
    ).astype(BF)


def lay_out_kernel(h1, mixed, h2, active, index_a, index_b, index_c, mine, send, pick):
    def put(value, at, count):
        mine[at : at + count, :] = value[:count].astype(BF)
        send[at : at + count, :] = value[count:].astype(BF)

    pick[0:D, :] = one_hot(index_a)
    put(dot(pick[0:D, :], h1[...], NT), H1A, 640)
    put(dot(pick[0:D, :], h2[...], NT), H2A, 640)
    pick[...] = one_hot(index_b)
    put(dot(pick[...], h1[...], NT), H1B, 768)
    put(dot(pick[...], mixed[...], NT), MIXB, 768)
    pick[0:D, :] = one_hot(index_c)
    for q in range(4):
        value = dot(pick[0:D, :], active[:, q * D : q * D + D], NT).astype(BF)
        for block in range(8):
            z, y = 2 * (q % 2) + block // 4, block % 4
            at = ACT + (y * 4 + z) * 80 if q < 2 else ACT + 1280 + (z * 4 + y) * 80
            mine[at : at + 80, :] = value[block * 80 : block * 80 + 80]
            send[at : at + 80, :] = value[640 + block * 80 : 720 + block * 80]


def parts_of(groups, half):
    group = half // 2
    starts = []
    for p in range(2):
        sent = groups[p]
        starts.append(pl.multiple_of(p * half + sent * group, 16))
        starts.append(pl.multiple_of(p * half + (1 - sent) * group, 16))
    return starts


class Copies:
    def __init__(self, sems):
        self.sems = sems
        self.count = 0

    def make(self, src, dst):
        copy = pltpu.make_async_copy(src, dst, self.sems.at[self.count])
        self.count += 1
        return copy

    def start(self, src, dst):
        copy = self.make(src, dst)
        copy.start()
        return copy


def finish(copies):
    for copy in copies:
        copy.wait()


def rows_of(refs, starts, group):
    return jnp.concatenate(
        [
            jnp.concatenate([ref[pl.ds(at, group), :] for at in starts], axis=0)
            for ref in refs
        ],
        axis=1,
    )


def product(left, refs, cols):
    return dot(left, jnp.concatenate([ref[:, cols] for ref in refs], axis=0))


def columns_job(copies, lines, starts, group, sources, outs, buffers, waits, extra=None):
    left = rows_of(lines, starts, group)
    done = []
    width = outs[0].shape[1]
    for n in range(0, width, 256):
        if n in waits:
            finish(waits[n])
        value = product(left, sources, slice(n, n + 256))
        if extra is not None and n == 0:
            value = value + jnp.concatenate([extra[pl.ds(at, group), :] for at in starts], axis=0)
        for i, buffer in enumerate(buffers):
            buffer[:, n : n + 256] = value[i * group : i * group + group].astype(BF)
        if (n + 256) % D == 0:
            cols = pl.ds(n + 256 - D, D)
            done += [copies.start(b.at[:, cols], o.at[:, cols]) for b, o in zip(buffers, outs)]
    return done


def up_down_grad_kernel(
    ints, groups_up, groups_down, mine, got, du, du_got, arriving, cot, arriving_got, cot_got,
    *rest,
):
    up_outs, down_outs, rest = rest[:4], rest[4:8], rest[8:]
    up_lines, down_lines, up_b, down_b, rest = rest[:2], rest[2:4], rest[4:6], rest[6:8], rest[8:]
    up_buffers, down_buffers, sems = rest[:4], rest[4:8], rest[8]
    copies = Copies(sems)
    first = [
        copies.start(src.at[pl.ds(ACT, 2560)], ref) for src, ref in zip((mine, got), down_lines)
    ]
    chosen = [copies.make(src, ref) for src, ref in zip((arriving, arriving_got), down_b)]
    others = [
        pltpu.make_async_copy(src, ref, sems.at[2 + i])
        for i, (src, ref) in enumerate(zip((cot, cot_got), down_b))
    ]

    @pl.when(ints[3] == 0)
    def _():
        for copy in chosen:
            copy.start()

    @pl.when(ints[3] != 0)
    def _():
        for copy in others:
            copy.start()

    lines = [copies.start(src.at[pl.ds(H2A, 640)], ref) for src, ref in zip((mine, got), up_lines)]
    waits = {
        n: [
            copies.start(src.at[:, pl.ds(n, D)], ref.at[:, pl.ds(n, D)])
            for src, ref in zip((du, du_got), up_b)
        ]
        for n in range(0, FF, D)
    }
    finish(first + chosen)
    done = []
    for at, buffer, out in zip(parts_of(groups_down, 1280), down_buffers, down_outs):
        left = rows_of(down_lines, [at], 640)
        for n in range(0, D, 256):
            buffer[:, n : n + 256] = product(left, down_b, slice(n, n + 256)).astype(BF)
        done.append(copies.start(buffer, out))
    finish(lines)
    done += columns_job(
        copies, up_lines, parts_of(groups_up, 320), 160, up_b, up_outs, up_buffers, waits
    )
    finish(done)


def attention_grad_kernel(groups_qk, groups_vo, mine, got, joint, joint_got, extra, *rest):
    qk_outs, vo_outs, rest = rest[:4], rest[4:8], rest[8:]
    qk_lines, v_lines, o_lines, b, rest = rest[:2], rest[2:4], rest[4:6], rest[6:8], rest[8:]
    qk_buffers, vo_buffers, sems = rest[:4], rest[4:8], rest[8]
    copies = Copies(sems)
    sources = (mine, got)
    loads = []
    for lines, base, chunks in (
        (v_lines, H1B, (2,)), (o_lines, MIXB, (3,)), (qk_lines, H1A, (0, 1))
    ):
        load = [
            copies.start(src.at[pl.ds(base, ref.shape[0])], ref) for src, ref in zip(sources, lines)
        ]
        for chunk in chunks:
            cols = pl.ds(chunk * D, D)
            load += [
                copies.start(src.at[pl.ds(0, ROWS), cols], ref.at[:, cols])
                for src, ref in zip((joint, joint_got), b)
            ]
        loads.append(load)
    done = []
    starts = parts_of(groups_vo, 384)
    for i, (lines, load) in enumerate(((v_lines, loads[0]), (o_lines, loads[1]))):
        cols = pl.ds(i * D, D)
        finish(load)
        done += columns_job(
            copies, lines, starts, 192, [ref.at[:, pl.ds((2 + i) * D, D)] for ref in b],
            [o.at[:, cols] for o in vo_outs], [v.at[:, cols] for v in vo_buffers], {},
            extra if i == 0 else None,
        )
    finish(loads[2])
    done += columns_job(
        copies, qk_lines, parts_of(groups_qk, 320), 160, b, qk_outs, qk_buffers, {}
    )
    finish(done)


VM = pl.BlockSpec(memory_space=pltpu.VMEM)
SM = pl.BlockSpec(memory_space=pltpu.SMEM)
HB = pl.BlockSpec(memory_space=pltpu.HBM)
LIMIT = 60 * 1024 * 1024


def call(kernel, ins, specs, outs, scratch, flops, moved):
    return pl.pallas_call(
        kernel,
        out_shape=tuple(
            (pltpu.HBM if o[2] is HB else jax.ShapeDtypeStruct)(*o[:2]) if isinstance(o, tuple) else o
            for o in outs
        ),
        in_specs=specs,
        out_specs=tuple(o[2] if isinstance(o, tuple) else VM for o in outs),
        scratch_shapes=scratch,
        compiler_params=pltpu.CompilerParams(vmem_limit_bytes=LIMIT),
        cost_estimate=pl.CostEstimate(flops=flops, bytes_accessed=moved, transcendentals=0),
    )(*ins)


def dma(n):
    return pltpu.SemaphoreType.DMA((n,))


TOKENS = ((ROWS, D), BF)
WIDE = ((ROWS, D), F32)
QKV = ((ROWS, 3 * D), BF)
PROB = ((20, 2 * SEQ, SEQ), BF)
HIDDEN = ((ROWS, FF), BF)
SUMS = ((2, D), F32)
ATT_W = pltpu.VMEM((D, 4 * D), BF)
UP_W = pltpu.VMEM((D, FF), BF)
DOWN_W = pltpu.VMEM((FF, D), BF)


def vmem(kind):
    return pltpu.VMEM(*kind)


def forward(ints, x, norms, weights):
    return call(
        forward_kernel,
        (ints, x, *norms, *weights),
        [SM] + [VM] * 5 + [HB] * 7,
        [TOKENS + (VM,)],
        [ATT_W, UP_W, DOWN_W]
        + [vmem(k) for k in (QKV, TOKENS, WIDE, TOKENS, TOKENS, HIDDEN)]
        + [dma(12)],
        6 * ROWS * D * FF, 40 * 2**20,
    )[0]


def both_ways(ints, x0, arriving, grad, norms, weights):
    kinds = (TOKENS, TOKENS, QKV, PROB, TOKENS, WIDE, TOKENS, HIDDEN, HIDDEN)
    return call(
        both_ways_kernel,
        (ints, x0, arriving, grad, *norms, *weights),
        [SM] + [VM] * 7 + [HB] * 7,
        [TOKENS + (VM,), TOKENS + (VM,)] + [k + (HB,) for k in kinds],
        [ATT_W, UP_W, DOWN_W] + [vmem(k) for k in kinds] + [vmem(WIDE), dma(12), dma(9)],
        12 * ROWS * D * FF, 60 * 2**20,
    )


def mlp_backward(ints, arriving, cot, slope, middle, g2, weights):
    return call(
        mlp_backward_kernel,
        (ints, arriving, cot, g2, slope, middle, *weights[2:]),
        [SM, VM, VM, VM] + [HB] * 7,
        [HIDDEN + (HB,), WIDE + (VM,), TOKENS + (VM,), SUMS + (VM,)],
        [
            UP_W, DOWN_W, vmem(TOKENS), vmem(WIDE), vmem(HIDDEN), vmem(WIDE), vmem(HIDDEN),
            dma(12), dma(17),
        ],
        2**20, 2**16,
    )


def heads_backward(ints, low, qkv, prob, weights):
    wout, oth = weights[1], weights[-1]
    return call(
        heads_backward_kernel,
        (ints, low, qkv, prob, wout, oth),
        [SM, VM] + [HB] * 4,
        [HIDDEN + (VM,)],
        [ATT_W, vmem(TOKENS), vmem(QKV), vmem(PROB), dma(4), dma(2)],
        2**20, 2**16,
    )[0]


def norm_one_backward(ints, g1, joint, dmiddle, x, weights):
    wqkv, oth = weights[0], weights[-1]
    return call(
        norm_one_backward_kernel,
        (ints, g1, joint, dmiddle, x, wqkv, oth),
        [SM, VM, VM] + [HB] * 4,
        [TOKENS + (VM,), SUMS + (VM,)],
        [ATT_W, vmem(WIDE), vmem(WIDE), vmem(TOKENS), dma(4), dma(2)],
        2**20, 2**16,
    )


def lay_out(h1, mixed, h2, active, indices):
    return call(
        lay_out_kernel,
        (h1, mixed, h2, active, *indices),
        [VM] * 7,
        [((LINES, ROWS), BF, VM), ((LINES, ROWS), BF, VM)],
        [pltpu.VMEM((1536, D), BF)],
        2**20, 2**16,
    )


def lines(count):
    return [pltpu.VMEM((count, ROWS), BF)] * 2


def up_down_grad(ints, groups, mine, got, du, du_got, grads):
    up, down = ((160, FF), BF), ((640, D), BF)
    outs = call(
        up_down_grad_kernel,
        (ints, groups[0], groups[1], mine, got, du, du_got, *grads),
        [SM] * 3 + [HB] * 8,
        [up + (HB,)] * 4 + [down + (HB,)] * 4,
        lines(640) + lines(2560) + [vmem(HIDDEN)] * 2 + [vmem(TOKENS)] * 2
        + [vmem(up)] * 4 + [vmem(down)] * 4 + [dma(40)],
        2**20, 2**16,
    )
    return outs[:4], outs[4:]


def attention_grad(groups, mine, got, joint, joint_got, extra):
    qk, vo = ((160, 2 * D), BF), ((192, 2 * D), BF)
    outs = call(
        attention_grad_kernel,
        (groups[0], groups[1], mine, got, joint, joint_got, extra),
        [SM] * 2 + [HB] * 4 + [VM],
        [qk + (HB,)] * 4 + [vo + (HB,)] * 4,
        lines(640) + lines(768) + lines(768) + [vmem(HIDDEN)] * 2
        + [vmem(qk)] * 4 + [vmem(vo)] * 4 + [dma(40)],
        2**20, 2**16,
    )
    return outs[:4], outs[4:]


def dp_pairs(move):
    pairs = []
    for z in range(4):
        for y in range(4):
            for c in range(2):
                to = move(z, y, c)
                pairs.append((z * 8 + y * 2 + c, to[0] * 8 + to[1] * 2 + to[2]))
    return pairs


FLIPS = {
    ("y", 1): dp_pairs(lambda z, y, c: (z, y ^ 1, c)),
    ("y", 3): dp_pairs(lambda z, y, c: (z, y ^ 3, c)),
    ("z", 1): dp_pairs(lambda z, y, c: (z ^ 1, y, c)),
    ("z", 3): dp_pairs(lambda z, y, c: (z ^ 3, y, c)),
}
CORE = dp_pairs(lambda z, y, c: (z, y, 1 - c))
SWAP = [(0, 1), (1, 0)]
ORDERS = ((0, 3, 1, 2), (0, 1, 2, 3))


def add_low(a, b):
    return (a.astype(F32) + b.astype(F32)).astype(BF)


def layout_rows(spacing, parity, core):
    order = ORDERS[parity]
    rows = []
    for c in (core, 1 - core):
        for p in range(2):
            for first in order:
                for second in order:
                    y, z = (first, second) if p == 0 else (second, first)
                    start = p * 640 + z * 160 + y * 40 + c * 20
                    rows += [start + i if i < 20 else -1 for i in range(spacing)]
    return np.array(rows, np.int32)


def block_rows(core):
    rows = []
    for c in (core, 1 - core):
        for block in range(8):
            rows += [block * 160 + c * 80 + i for i in range(80)]
    return np.array(rows, np.int32)


LAYOUTS = (
    (layout_rows(20, 0, 0), layout_rows(20, 0, 1)),
    (layout_rows(24, 1, 0), layout_rows(24, 1, 1)),
    (block_rows(0), block_rows(1)),
)


def picks_of(parity, at):
    if parity == 0:
        return jnp.where((at == 0) | (at == 3), 0, 1), at // 2
    return at // 2, at % 2


def flips_of(parity):
    return (1, 3) if parity == 0 else (3, 1)


class Flights:
    WINDOW = 5

    def __init__(self):
        self.gots = []

    def send(self, value, axis, flip):
        if len(self.gots) >= self.WINDOW:
            value, _ = lax.optimization_barrier((value, self.gots[-self.WINDOW]))
        got = (
            lax.ppermute(value, "pair", SWAP)
            if axis == "x"
            else lax.ppermute(value, "dp", FLIPS[axis, flip])
        )
        self.gots.append(got)
        return got


class Rings:
    def __init__(self, flights, send, keep, axes, parity, at):
        self.flights, self.to_send, self.keep = flights, send, keep
        self.plan = [
            (axis, flip, pick)
            for axis in axes
            for flip, pick in zip(flips_of(parity), picks_of(parity, at[axis]))
        ]
        self.step = 0

    def start(self):
        axis, flip, _ = self.plan[self.step]
        self.got = self.flights.send(self.to_send, axis, flip)
        self.step += 1

    def finish(self):
        value = add_low(self.keep, self.got)
        if self.step < 4:
            self.split(value)
        return value

    def finish_first(self):
        return add_low(self.keep, self.got)

    def split(self, value):
        pick = self.plan[self.step][2]
        half = value.shape[0] // 2
        self.to_send = lax.dynamic_slice_in_dim(value, (1 - pick) * half, half, 0)
        self.keep = lax.dynamic_slice_in_dim(value, pick * half, half, 0)


def join_up(up, qk):
    return jnp.concatenate([up, qk], axis=1)


def join_down(down, vo):
    return jnp.concatenate(
        [down.reshape(4, 80, D), vo[:, :D].reshape(4, 24, D), vo[:, D:].reshape(4, 24, D)], axis=1
    ).reshape(-1, D)


def over_pair(flights, values, pair):
    send = jnp.where(pair == 0, values[1], values[0])
    keep = jnp.where(pair == 0, values[0], values[1])
    return keep.astype(F32) + flights.send(send, "x", 1).astype(F32)


def sums_rows(sums):
    t = sums.reshape(4, 2, 4, 4, 2, 20)
    first = jnp.transpose(t[:, 0], (2, 1, 3, 0, 4)).reshape(1, 16, 1, 160)
    second = jnp.transpose(t[:, 1], (1, 2, 3, 0, 4)).reshape(1, 16, 1, 160)
    t = jnp.concatenate([first, second], axis=0)
    return jnp.pad(t, ((0, 0), (0, 0), (20, 3), (0, 96))).reshape(768, 256)


def shards(
    tokens, lengths, cotangent, w_qkv, w_out, w_up, w_down,
    norm1_gain, norm1_bias, norm2_gain, norm2_bias,
):
    section = lax.axis_index("section")
    pair = lax.axis_index("pair")
    place = lax.axis_index("dp")
    at = {"z": place // 8, "y": (place // 2) % 4}
    core = place % 2
    swap = lambda v: lax.ppermute(v, "dp", CORE)
    ints = jnp.concatenate(
        [
            pair[None].astype(jnp.int32), lengths[:, 0],
            section[None].astype(jnp.int32), core[None].astype(jnp.int32),
        ]
    )
    groups = [
        jnp.stack([1 - picks_of(k, at["y"])[0], 1 - picks_of(k, at["z"])[0]]).astype(jnp.int32)
        for k in range(2)
    ]
    indices = [jnp.where(core == 0, a, b)[:, None] for a, b in LAYOUTS]
    norms = (norm1_gain, norm1_bias, norm2_gain, norm2_bias)
    x0 = tokens.reshape(ROWS, D)
    cot = cotangent.reshape(ROWS, D)
    cot_got = swap(cot)
    wqkv, wout, wup, wdown = w_qkv[0], w_out[0], w_up[0], w_down[0]

    row = (place % 8) * PIECE
    att_piece = jnp.where(
        at["z"] == 3,
        lax.dynamic_slice(wout, (row, 0), (PIECE, D)),
        lax.dynamic_slice(wqkv, (row, jnp.minimum(at["z"], 2) * D), (PIECE, D)),
    )
    piece = jnp.concatenate(
        [
            att_piece,
            lax.dynamic_slice(wup, (row, at["z"] * D), (PIECE, D)),
            lax.dynamic_slice(wdown, (DIRECT + place * TAIL, 0), (TAIL, D)),
        ],
        axis=0,
    )
    piece = lax.ppermute(piece, "pair", SWAP)
    half = lax.dynamic_slice(wdown, (core * (DIRECT // 2), 0), (DIRECT // 2, D))
    half, piece = lax.optimization_barrier((half, piece))
    oth = lax.all_gather(piece, "dp", axis=0)
    near = lax.ppermute(half, "pair", SWAP)
    far = swap(near)

    ints, groups, indices, cot_got, oth, near, far = lax.optimization_barrier(
        (ints, groups, indices, cot_got, oth, near, far)
    )
    weights = (wqkv, wout, wup, wdown, near, far, oth)
    y = forward(ints, x0, norms, weights)
    arriving = lax.ppermute(y, "section", [(0, 1)])
    y, dx, x, h1, qkv, prob, mixed, middle, h2, active, slope = both_ways(
        ints, x0, arriving, cot, norms, weights
    )
    arriving = lax.ppermute(dx, "section", [(1, 0)])

    mine, send = lay_out(h1, mixed, h2, active, indices)
    got = swap(send)
    arriving, got = lax.optimization_barrier((arriving, got))
    arriving_got = swap(arriving)
    du, dmiddle, low, sums_two = mlp_backward(
        ints, arriving, cot, slope, middle, norm2_gain, weights
    )
    du, low, arriving_got = lax.optimization_barrier((du, low, arriving_got))
    grads = (arriving, cot, arriving_got, cot_got)
    du_got = swap(du)
    joint = heads_backward(ints, low, qkv, prob, weights)
    joint_got = swap(joint)
    joint, du, du_got, grads = lax.optimization_barrier((joint, du, du_got, grads))
    d_up, d_down = up_down_grad(ints, groups, mine, got, du, du_got, grads)
    joint, dmiddle, d_down = lax.optimization_barrier((joint, dmiddle, d_down))
    dx, sums_one = norm_one_backward(ints, norm1_gain, joint, dmiddle, x, weights)
    dx, sums_one, joint, joint_got, place, pair = lax.optimization_barrier(
        (dx, sums_one, joint, joint_got, place, pair)
    )
    at = {"z": place // 8, "y": (place // 2) % 4}
    extra = sums_rows(jnp.concatenate([sums_one, sums_two], axis=0))
    d_qk, d_vo = attention_grad(groups, mine, got, joint, joint_got, extra)
    keeps = [d[i] for d in (d_up, d_down, d_vo, d_qk) for i in (1, 3)]
    keeps = lax.optimization_barrier(keeps)
    d_up, d_down, d_vo, d_qk = (
        (d[0], keeps[2 * i], d[2], keeps[2 * i + 1])
        for i, d in enumerate((d_up, d_down, d_vo, d_qk))
    )

    flights = Flights()

    def rings(parts, parity):
        return [
            Rings(flights, parts[0], parts[1], "yz", parity, at),
            Rings(flights, parts[2], parts[3], "zy", parity, at),
        ]

    def each(method, group):
        return [getattr(r, method)() for r in group]

    down, up, vo, qk = rings(d_down, 1), rings(d_up, 0), rings(d_vo, 1), rings(d_qk, 0)
    def phase(now, later):
        each("start", now)
        gots, sends = lax.optimization_barrier(
            ([r.got for r in now], [r.to_send for r in later])
        )
        for r, v in zip(now, gots):
            r.got = v
        for r, v in zip(later, sends):
            r.to_send = v

    phase(down + up, vo + qk)
    each("finish", down + up)
    phase(vo + qk, down + up)
    each("finish", vo + qk)
    phase(down + up, vo + qk)
    each("start", vo + qk)
    for one, two, join in ((down, vo, join_down), (up, qk, join_up)):
        for a, b in zip(one, two):
            value = join(a.finish_first(), b.finish_first())
            a.split(value)
    each("start", down + up)
    each("finish", down + up)
    each("start", down + up)
    g_down = over_pair(flights, each("finish", down), pair)
    g_up = over_pair(flights, each("finish", up), pair)
    sums = g_down[100, :160].reshape(2, 80)
    sums = (
        lax.dynamic_index_in_dim(sums, place % 2, 0, keepdims=False)
        + swap(lax.dynamic_index_in_dim(sums, 1 - place % 2, 0, keepdims=False))
    ).reshape(4, 20)
    return (
        y.reshape(1, 2, 1, SEQ, D),
        dx.reshape(1, 2, 1, SEQ, D),
        jnp.concatenate([g_up[:, FF:], g_down[80:100]], axis=1)[None],
        g_down[104:124][None],
        g_up[:, :FF][None],
        g_down[:80][None],
        sums[0:1],
        sums[1:2],
        sums[2:3],
        sums[3:4],
    )


def solution(mesh):
    rows = ("pair", "dp")
    in_specs = (
        P(None, rows, None, None),
        P(None, rows),
        P(None, rows, None, None),
        P("section", "pair", None),
        P("section", "pair", None),
        P("section", "pair", None),
        P("section", "pair", None),
        P("section", None),
        P("section", None),
        P("section", None),
        P("section", None),
    )
    out_specs = (
        P("section", None, rows, None, None),
        P("section", None, rows, None, None),
        P("section", rows, None),
        P("section", rows, None),
        P("section", rows, None),
        P("section", rows, None),
        P("section", rows),
        P("section", rows),
        P("section", rows),
        P("section", rows),
    )
    return jax.shard_map(shards, mesh=mesh, in_specs=in_specs, out_specs=out_specs, check_vma=False)
```

```python
import jax
import jax.numpy as jnp
import numpy as np
from jax import lax
from jax.experimental import pallas as pl
from jax.experimental.pallas import tpu as pltpu
from jax.sharding import PartitionSpec as P

D = 1280
FF = 5120
SEQ = 128
ROWS = 2 * SEQ
EPSILON = 1e-05
BF = jnp.bfloat16
F32 = jnp.float32
PIECE = 80

NN = (((1,), (0,)), ((), ()))
NT = (((1,), (1,)), ((), ()))
TN = (((0,), (0,)), ((), ()))


def dot(a, b, dims=NN):
    return lax.dot_general(a, b, dims, preferred_element_type=F32)


def row_blocks(count, body):
    def step(i, carry):
        body(pl.ds(pl.multiple_of(i * 32, 32), 32))
        return carry

    lax.fori_loop(0, count // 32, step, 0, unroll=4)


def tiles(body):
    def step(i, carry):
        body(pl.ds(pl.multiple_of(i * 256, 256), 256))
        return carry

    lax.fori_loop(0, D // 256, step, 0)


def stats(v):
    mean = jnp.mean(v, axis=-1, keepdims=True)
    centred = v - mean
    rstd = lax.rsqrt(jnp.mean(centred * centred, axis=-1, keepdims=True) + EPSILON)
    return centred * rstd, rstd


AHEAD = 3


class Stream:
    def __init__(self):
        self.blocks = []
        self.started = 0

    def add(self, name, copies, target, sem):
        self.blocks.append((name, copies, target, sem))

    def begin(self, upto=AHEAD):
        while self.started < min(upto, len(self.blocks)):
            for copy in self.blocks[self.started][1]():
                copy.start()
            self.started += 1

    def need(self, name):
        at = [block[0] for block in self.blocks].index(name)
        self.begin(at + 1 + AHEAD)
        _, _, target, sem = self.blocks[at]
        pltpu.make_async_copy(target, target, sem).wait()


def square(pair, own, oth, which, dst, col, sem, group):
    def copies():
        yield pltpu.make_async_copy(
            own, dst.at[pl.ds(pl.multiple_of(pair * 640, 640), 640), pl.ds(col, D)], sem
        )
        for r in range(8):
            row = pl.multiple_of((1 - pair) * 640 + r * PIECE, PIECE)
            yield pltpu.make_async_copy(
                oth.at[group * 8 + r, pl.ds(which * PIECE, PIECE)],
                dst.at[pl.ds(row, PIECE), pl.ds(col, D)],
                sem,
            )

    return copies


def add_attention(stream, pair, wqkv, wout, oth, dst, sems, order):
    for g in order:
        own = wqkv.at[:, pl.ds(g * D, D)] if g < 3 else wout
        copies = square(pair, own, oth, 0, dst, g * D, sems.at[g], g)
        stream.add(("att", g), copies, dst.at[:, pl.ds(g * D, D)], sems.at[g])


def add_up(stream, pair, wup, oth, dst, sems):
    for g in range(4):
        copies = square(pair, wup.at[:, pl.ds(g * D, D)], oth, 1, dst, g * D, sems.at[4 + g], g)
        stream.add(("up", g), copies, dst.at[:, pl.ds(g * D, D)], sems.at[4 + g])


DIRECT, TAIL = 2048, 16
DOWN_BLOCKS = ((True, 0, 1280), (True, 1280, 1280), (False, 0, DIRECT), (False, DIRECT, 512))


def down_row(pair, block, n=0):
    own, start, _ = DOWN_BLOCKS[block]
    return pl.multiple_of((pair if own else 1 - pair) * 2560 + start + n, 256)


def add_down(stream, pair, core, wdown, near, far, oth, dst, sems):
    def own(block):
        _, start, rows = DOWN_BLOCKS[block]
        yield pltpu.make_async_copy(
            wdown.at[pl.ds(start, rows)],
            dst.at[pl.ds(down_row(pair, block), rows)],
            sems.at[8 + block],
        )

    def direct():
        half = DIRECT // 2
        for source, part in ((near, core), (far, 1 - core)):
            row = pl.multiple_of((1 - pair) * 2560 + part * half, half // 2)
            yield pltpu.make_async_copy(source, dst.at[pl.ds(row, half)], sems.at[10])

    def tail():
        for d in range(32):
            row = pl.multiple_of((1 - pair) * 2560 + DIRECT + d * TAIL, TAIL)
            yield pltpu.make_async_copy(
                oth.at[d, pl.ds(2 * PIECE, TAIL)], dst.at[pl.ds(row, TAIL)], sems.at[11]
            )

    plans = (lambda: own(0), lambda: own(1), direct, tail)
    for block, copies in enumerate(plans):
        target = dst.at[pl.ds(0, DOWN_BLOCKS[block][2])]
        stream.add(("down", block), copies, target, sems.at[8 + block])


def forward_attention(ints, x_ref, norms, w_ref, need, qkv_ref, prob_ref, mixed_ref, middle_ref, h1_ref, h2_ref, done):
    g1, b1, g2, b2 = norms

    def norm_one(rows):
        hat, _ = stats(x_ref[rows, :].astype(F32))
        h1_ref[rows, :] = (hat * g1[...] + b1[...]).astype(BF)

    row_blocks(ROWS, norm_one)
    done("h1")
    for g in range(3):
        need(("att", g))
        for n in range(g * D, g * D + D, 256):
            qkv_ref[:, n : n + 256] = dot(h1_ref[...], w_ref[:, n : n + 256]).astype(BF)
    done("qkv")
    low = lax.broadcasted_iota(jnp.int32, (SEQ, 128), 1) < 64
    zero = jnp.zeros((SEQ, 128), BF)
    key_at = lax.broadcasted_iota(jnp.int32, (2 * SEQ, SEQ), 1)

    def split(v):
        return jnp.concatenate([jnp.where(low, v, zero), jnp.where(low, zero, v)], axis=0)

    for s in range(2):
        valid = key_at < ints[1 + s]
        rows = pl.ds(s * SEQ, SEQ)

        def heads(i, carry):
            at = pl.multiple_of(i * 128, 128)
            q = qkv_ref[rows, pl.ds(at, 128)] * jnp.asarray(0.125, BF)
            k = qkv_ref[rows, pl.ds(at + D, 128)]
            v = qkv_ref[rows, pl.ds(at + 2 * D, 128)]
            scores = jnp.where(valid, dot(split(q), k, NT), -1e30)
            raised = jnp.exp(scores - jnp.max(scores, axis=-1, keepdims=True))
            prob = (raised / jnp.sum(raised, axis=-1, keepdims=True)).astype(BF)
            if prob_ref is not None:
                prob_ref[s * 10 + i] = prob
            side = jnp.concatenate([prob[:SEQ], prob[SEQ:]], axis=1)
            mixed_ref[rows, pl.ds(at, 128)] = dot(side, split(v)).astype(BF)
            return carry

        lax.fori_loop(0, 10, heads, 0, unroll=10)
    done("prob")
    done("mixed")
    need(("att", 3))
    for n in range(0, D, 256):
        middle_ref[:, n : n + 256] = x_ref[:, n : n + 256].astype(F32) + dot(
            mixed_ref[...], w_ref[:, 3 * D + n : 3 * D + n + 256]
        )
    done("middle")

    def norm_two(rows):
        hat, _ = stats(middle_ref[rows, :])
        h2_ref[rows, :] = (hat * g2[...] + b2[...]).astype(BF)

    row_blocks(ROWS, norm_two)
    done("h2")


def forward_mlp(h2_ref, middle_ref, wu_ref, wd_ref, need, y_ref, active_ref, slope_ref, done):
    for g in range(4):
        need(("up", g))
        for n in range(g * D, g * D + D, 256):
            u = dot(h2_ref[...], wu_ref[:, n : n + 256])
            cdf = 0.5 + 0.5 * lax.erf(u * 0.7071067811865476)
            active_ref[:, n : n + 256] = (u * cdf).astype(BF)
            if slope_ref is not None:
                pdf = 0.3989422804014327 * jnp.exp(-0.5 * u * u)
                slope_ref[:, n : n + 256] = (cdf + u * pdf).astype(BF)
    done("active")
    done("slope")
    for g in range(4):
        need(("down", g))

    def columns(at):
        y_ref[:, at] = (middle_ref[:, at] + dot(active_ref[...], wd_ref[:, at])).astype(BF)

    tiles(columns)


def nothing_done(name):
    pass


def forward_kernel(
    ints, x_ref, g1, b1, g2, b2, wqkv, wout, wup, wdown, near, far, oth, y_ref,
    w_ref, wu_ref, wd_ref, qkv_ref, mixed_ref, middle_ref, h1_ref, h2_ref, active_ref, sems,
):
    stream = Stream()
    add_attention(stream, ints[0], wqkv, wout, oth, w_ref, sems, range(4))
    add_up(stream, ints[0], wup, oth, wu_ref, sems)
    add_down(stream, ints[0], ints[4], wdown, near, far, oth, wd_ref, sems)
    stream.begin()
    forward_attention(
        ints, x_ref, (g1, b1, g2, b2), w_ref, stream.need,
        qkv_ref, None, mixed_ref, middle_ref, h1_ref, h2_ref, nothing_done,
    )
    forward_mlp(
        h2_ref, middle_ref, wu_ref, wd_ref, stream.need, y_ref, active_ref, None, nothing_done
    )


def fold(total, value):
    for r in range(0, 32, 8):
        total = total + value[r : r + 8]
    return total


def norm_backward(grad_ref, value_of, gain, write, sums_ref):
    nothing = jnp.zeros((8, D), F32)

    def step(i, carry):
        of_gain, of_bias = carry
        rows = pl.ds(pl.multiple_of(i * 32, 32), 32)
        hat, rstd = stats(value_of(rows))
        grad = grad_ref[rows, :]
        scaled = grad * gain[...]
        first = jnp.mean(scaled, axis=-1, keepdims=True)
        second = jnp.mean(scaled * hat, axis=-1, keepdims=True)
        write(rows, rstd * (scaled - first - hat * second))
        return fold(of_gain, grad * hat), fold(of_bias, grad)

    of_gain, of_bias = lax.fori_loop(0, ROWS // 32, step, (nothing, nothing), unroll=4)
    if sums_ref is not None:
        sums_ref[0:1, :] = jnp.sum(of_gain, axis=0, keepdims=True)
        sums_ref[1:2, :] = jnp.sum(of_bias, axis=0, keepdims=True)


def backward_mlp(pair, grad_ref, slope_ref, middle_ref, g2, wu_ref, wd_ref, dh_ref, du_ref, dmiddle_ref, low_ref, sums_ref, before=nothing_done, done=nothing_done):
    for block in range(4):
        before(block)
        for n in range(0, DOWN_BLOCKS[block][2], 256):
            at = pl.ds(down_row(pair, block, n), 256)
            dact = dot(grad_ref[...], wd_ref[at, :], NT)
            du_ref[:, at] = (dact * slope_ref[:, at].astype(F32)).astype(BF)
        done(block)
    before("up")

    def features(at):
        dh_ref[:, at] = dot(du_ref[...], wu_ref[at, :], NT)

    tiles(features)

    def write(rows, grad):
        total = grad_ref[rows, :].astype(F32) + grad
        dmiddle_ref[rows, :] = total
        low_ref[rows, :] = total.astype(BF)

    before("middle")
    norm_backward(dh_ref, lambda rows: middle_ref[rows, :], g2, write, sums_ref)


def backward_heads(low_ref, qkv_ref, prob_ref, w_ref, dmixed_ref, dq, dk, dv, before=nothing_done):
    before("out")
    for n in range(0, D, 256):
        dmixed_ref[:, n : n + 256] = dot(
            low_ref[...], w_ref[n : n + 256, 3 * D : 4 * D], NT
        ).astype(BF)
    before("heads")
    low = lax.broadcasted_iota(jnp.int32, (SEQ, 128), 1) < 64
    zero = jnp.zeros((SEQ, 128), BF)

    def split(v):
        return jnp.concatenate([jnp.where(low, v, zero), jnp.where(low, zero, v)], axis=0)

    for s in range(2):
        rows = pl.ds(s * SEQ, SEQ)

        def heads(i, carry):
            at = pl.multiple_of(i * 128, 128)
            q = qkv_ref[rows, pl.ds(at, 128)] * jnp.asarray(0.125, BF)
            k = qkv_ref[rows, pl.ds(at + D, 128)] * jnp.asarray(0.125, BF)
            v = qkv_ref[rows, pl.ds(at + 2 * D, 128)]
            dm = split(dmixed_ref[rows, pl.ds(at, 128)])
            prob = prob_ref[s * 10 + i]
            dprob = dot(dm, v, NT)
            wide = prob.astype(F32)
            inner = jnp.sum(dprob * wide, axis=-1, keepdims=True)
            dscore = (wide * (dprob - inner)).astype(BF)
            side = jnp.concatenate([dscore[:SEQ], dscore[SEQ:]], axis=1)
            dq[rows, pl.ds(at, 128)] = dot(side, split(k)).astype(BF)
            dk[rows, pl.ds(at, 128)] = dot(dscore, split(q), TN).astype(BF)
            dv[rows, pl.ds(at, 128)] = dot(prob, dm, TN).astype(BF)
            return carry

        lax.fori_loop(0, 10, heads, 0, unroll=10)


def backward_norm_one(dmiddle_ref, dqkv, x_ref, g1, w_ref, dh_ref, dx_ref, sums_ref, before=nothing_done):
    before("qkv")

    def features(at):
        dh_ref[:, at] = dot(dqkv[...], w_ref[at, 0 : 3 * D], NT)

    tiles(features)

    def write(rows, grad):
        dx_ref[rows, :] = (dmiddle_ref[rows, :] + grad).astype(BF)

    before("norm")
    norm_backward(dh_ref, lambda rows: x_ref[rows, :].astype(F32), g1, write, sums_ref)


KEPT = ("x", "h1", "qkv", "prob", "mixed", "middle", "h2", "active", "slope")


def both_ways_kernel(
    ints, x0, arriving, grad_ref, g1, b1, g2, b2, wqkv, wout, wup, wdown, near, far, oth,
    y_ref, dx_ref, x_out, h1_out, qkv_out, prob_out, mixed_out, middle_out, h2_out, active_out, slope_out,
    w_ref, wu_ref, wd_ref, x_ref, h1_ref, qkv_ref, prob_ref, mixed_ref, middle_ref, h2_ref,
    active_ref, slope_ref, dh_ref, sems, kept_sems,
):
    stream = Stream()
    add_attention(stream, ints[0], wqkv, wout, oth, w_ref, sems, range(4))
    add_up(stream, ints[0], wup, oth, wu_ref, sems)
    add_down(stream, ints[0], ints[4], wdown, near, far, oth, wd_ref, sems)
    stream.begin()
    refs = dict(zip(KEPT, (x_ref, h1_ref, qkv_ref, prob_ref, mixed_ref, middle_ref, h2_ref, active_ref, slope_ref)))
    outs = dict(zip(KEPT, (x_out, h1_out, qkv_out, prob_out, mixed_out, middle_out, h2_out, active_out, slope_out)))

    def copy(name):
        return pltpu.make_async_copy(refs[name], outs[name], kept_sems.at[KEPT.index(name)])

    def done(name):
        copy(name).start()

    @pl.when(ints[3] == 0)
    def _():
        x_ref[...] = x0[...]

    @pl.when(ints[3] != 0)
    def _():
        x_ref[...] = arriving[...]

    done("x")
    forward_attention(
        ints, x_ref, (g1, b1, g2, b2), w_ref, stream.need,
        qkv_ref, prob_ref, mixed_ref, middle_ref, h1_ref, h2_ref, done,
    )
    forward_mlp(
        h2_ref, middle_ref, wu_ref, wd_ref, stream.need, y_ref, active_ref, slope_ref, done
    )
    for name in ("h1", "qkv", "mixed", "middle", "h2", "active"):
        copy(name).wait()
    backward_mlp(
        ints[0], grad_ref, slope_ref, middle_ref, g2, wu_ref, wd_ref, dh_ref, active_ref, middle_ref, h1_ref,
        None,
    )
    backward_heads(
        h1_ref, qkv_ref, prob_ref, w_ref, h2_ref,
        qkv_ref.at[:, pl.ds(0, D)], qkv_ref.at[:, pl.ds(D, D)], qkv_ref.at[:, pl.ds(2 * D, D)],
    )
    backward_norm_one(
        middle_ref, qkv_ref, x_ref, g1, w_ref, dh_ref, dx_ref, None
    )
    for name in ("x", "prob", "slope"):
        copy(name).wait()


def mlp_backward_kernel(
    ints, arriving, cot, g2, slope, middle, wup, wdown, near, far, oth, du_out, dmiddle_ref, low_ref, sums_ref,
    wu_ref, wd_ref, grad_ref, dh_ref, slope_ref, middle_ref, du_ref, sems, kept_sems,
):
    def part(block, source, target, sem):
        cols = pl.ds(down_row(ints[0], block), DOWN_BLOCKS[block][2])
        return pltpu.make_async_copy(source.at[:, cols], target.at[:, cols], sem)

    get_middle = pltpu.make_async_copy(middle, middle_ref, kept_sems.at[16])
    stream = Stream()
    add_down(stream, ints[0], ints[4], wdown, near, far, oth, wd_ref, sems)
    add_up(stream, ints[0], wup, oth, wu_ref, sems)

    def get_slope(g):
        return part(g, slope, slope_ref, kept_sems.at[g])

    def put_du(g):
        return part(g, du_ref, du_out, kept_sems.at[8 + g])

    for g in range(4):
        get_slope(g).start()
        if g < AHEAD:
            stream.begin(g + 1)
    get_middle.start()

    @pl.when(ints[3] == 0)
    def _():
        grad_ref[...] = arriving[...]

    @pl.when(ints[3] != 0)
    def _():
        grad_ref[...] = cot[...]


    def before(step):
        if step == "middle":
            get_middle.wait()
        elif step == "up":
            for g in range(4):
                stream.need(("up", g))
        else:
            get_slope(step).wait()
            stream.need(("down", step))

    def done(g):
        put_du(g).start()

    backward_mlp(
        ints[0], grad_ref, slope_ref, middle_ref, g2, wu_ref, wd_ref, dh_ref, du_ref, dmiddle_ref, low_ref,
        sums_ref, before, done,
    )
    for g in range(4):
        put_du(g).wait()


def heads_backward_kernel(
    ints, low_ref, qkv, prob, wout, oth, joint_ref,
    w_ref, dmixed_ref, qkv_ref, prob_ref, sems, kept_sems,
):
    stream = Stream()
    add_attention(stream, ints[0], None, wout, oth, w_ref, sems, (3,))
    stream.begin()
    kept = [
        pltpu.make_async_copy(src, dst, kept_sems.at[i])
        for i, (src, dst) in enumerate(((qkv, qkv_ref), (prob, prob_ref)))
    ]
    for copy in kept:
        copy.start()

    def before(name):
        if name == "out":
            stream.need(("att", 3))
        else:
            for copy in kept:
                copy.wait()

    joint_ref[:, 3 * D :] = low_ref[...]
    backward_heads(
        low_ref, qkv_ref, prob_ref, w_ref, dmixed_ref,
        *(joint_ref.at[:, pl.ds(i * D, D)] for i in range(3)), before,
    )


def norm_one_backward_kernel(
    ints, g1, joint_ref, dmiddle, x, wqkv, oth, dx_ref, sums_ref,
    w_ref, dh_ref, dmiddle_ref, x_ref, sems, kept_sems,
):
    stream = Stream()
    add_attention(stream, ints[0], wqkv, None, oth, w_ref, sems, range(3))
    stream.begin()
    kept = [
        pltpu.make_async_copy(src, dst, kept_sems.at[i])
        for i, (src, dst) in enumerate(((dmiddle, dmiddle_ref), (x, x_ref)))
    ]
    for copy in kept:
        copy.start()

    def before(name):
        if name == "qkv":
            for g in range(3):
                stream.need(("att", g))
        else:
            for copy in kept:
                copy.wait()

    backward_norm_one(
        dmiddle_ref, joint_ref.at[:, pl.ds(0, 3 * D)], x_ref, g1, w_ref, dh_ref,
        dx_ref, sums_ref, before,
    )


H1A, H1B, MIXB, H2A, ACT, LINES = 0, 640, 1408, 2176, 2816, 5376


def one_hot(index_ref):
    rows = index_ref.shape[0]
    return jnp.where(
        lax.broadcasted_iota(jnp.int32, (rows, D), 1) == index_ref[...], 1.0, 0.0
    ).astype(BF)


def lay_out_kernel(h1, mixed, h2, active, index_a, index_b, index_c, mine, send, pick):
    def put(value, at, count):
        mine[at : at + count, :] = value[:count].astype(BF)
        send[at : at + count, :] = value[count:].astype(BF)

    pick[0:D, :] = one_hot(index_a)
    put(dot(pick[0:D, :], h1[...], NT), H1A, 640)
    put(dot(pick[0:D, :], h2[...], NT), H2A, 640)
    pick[...] = one_hot(index_b)
    put(dot(pick[...], h1[...], NT), H1B, 768)
    put(dot(pick[...], mixed[...], NT), MIXB, 768)
    pick[0:D, :] = one_hot(index_c)
    for q in range(4):
        value = dot(pick[0:D, :], active[:, q * D : q * D + D], NT).astype(BF)
        for block in range(8):
            z, y = 2 * (q % 2) + block // 4, block % 4
            at = ACT + (y * 4 + z) * 80 if q < 2 else ACT + 1280 + (z * 4 + y) * 80
            mine[at : at + 80, :] = value[block * 80 : block * 80 + 80]
            send[at : at + 80, :] = value[640 + block * 80 : 720 + block * 80]


def parts_of(groups, half):
    group = half // 2
    starts = []
    for p in range(2):
        sent = groups[p]
        starts.append(pl.multiple_of(p * half + sent * group, 16))
        starts.append(pl.multiple_of(p * half + (1 - sent) * group, 16))
    return starts


class Copies:
    def __init__(self, sems):
        self.sems = sems
        self.count = 0

    def make(self, src, dst):
        copy = pltpu.make_async_copy(src, dst, self.sems.at[self.count])
        self.count += 1
        return copy

    def start(self, src, dst):
        copy = self.make(src, dst)
        copy.start()
        return copy


def finish(copies):
    for copy in copies:
        copy.wait()


def rows_of(refs, starts, group):
    return jnp.concatenate(
        [
            jnp.concatenate([ref[pl.ds(at, group), :] for at in starts], axis=0)
            for ref in refs
        ],
        axis=1,
    )


def product(left, refs, cols):
    return dot(left, jnp.concatenate([ref[:, cols] for ref in refs], axis=0))


def columns_job(copies, lines, starts, group, sources, outs, buffers, waits, extra=None):
    left = rows_of(lines, starts, group)
    done = []
    width = outs[0].shape[1]
    for n in range(0, width, 256):
        if n in waits:
            finish(waits[n])
        value = product(left, sources, slice(n, n + 256))
        if extra is not None and n == 0:
            value = value + jnp.concatenate([extra[pl.ds(at, group), :] for at in starts], axis=0)
        for i, buffer in enumerate(buffers):
            buffer[:, n : n + 256] = value[i * group : i * group + group].astype(BF)
        if (n + 256) % D == 0:
            cols = pl.ds(n + 256 - D, D)
            done += [copies.start(b.at[:, cols], o.at[:, cols]) for b, o in zip(buffers, outs)]
    return done


def up_down_grad_kernel(
    ints, groups_up, groups_down, mine, got, du, du_got, arriving, cot, arriving_got, cot_got,
    *rest,
):
    up_outs, down_outs, rest = rest[:4], rest[4:8], rest[8:]
    up_lines, down_lines, up_b, down_b, rest = rest[:2], rest[2:4], rest[4:6], rest[6:8], rest[8:]
    up_buffers, down_buffers, sems = rest[:4], rest[4:8], rest[8]
    copies = Copies(sems)
    first = [
        copies.start(src.at[pl.ds(ACT, 2560)], ref) for src, ref in zip((mine, got), down_lines)
    ]
    chosen = [copies.make(src, ref) for src, ref in zip((arriving, arriving_got), down_b)]
    others = [
        pltpu.make_async_copy(src, ref, sems.at[2 + i])
        for i, (src, ref) in enumerate(zip((cot, cot_got), down_b))
    ]

    @pl.when(ints[3] == 0)
    def _():
        for copy in chosen:
            copy.start()

    @pl.when(ints[3] != 0)
    def _():
        for copy in others:
            copy.start()

    lines = [copies.start(src.at[pl.ds(H2A, 640)], ref) for src, ref in zip((mine, got), up_lines)]
    waits = {
        n: [
            copies.start(src.at[:, pl.ds(n, D)], ref.at[:, pl.ds(n, D)])
            for src, ref in zip((du, du_got), up_b)
        ]
        for n in range(0, FF, D)
    }
    finish(first + chosen)
    done = []
    for at, buffer, out in zip(parts_of(groups_down, 1280), down_buffers, down_outs):
        left = rows_of(down_lines, [at], 640)
        for n in range(0, D, 256):
            buffer[:, n : n + 256] = product(left, down_b, slice(n, n + 256)).astype(BF)
        done.append(copies.start(buffer, out))
    finish(lines)
    done += columns_job(
        copies, up_lines, parts_of(groups_up, 320), 160, up_b, up_outs, up_buffers, waits
    )
    finish(done)


def attention_grad_kernel(groups_qk, groups_vo, mine, got, joint, joint_got, extra, *rest):
    qk_outs, vo_outs, rest = rest[:4], rest[4:8], rest[8:]
    qk_lines, v_lines, o_lines, b, rest = rest[:2], rest[2:4], rest[4:6], rest[6:8], rest[8:]
    qk_buffers, vo_buffers, sems = rest[:4], rest[4:8], rest[8]
    copies = Copies(sems)
    sources = (mine, got)
    loads = []
    for lines, base, chunks in (
        (v_lines, H1B, (2,)), (o_lines, MIXB, (3,)), (qk_lines, H1A, (0, 1))
    ):
        load = [
            copies.start(src.at[pl.ds(base, ref.shape[0])], ref) for src, ref in zip(sources, lines)
        ]
        for chunk in chunks:
            cols = pl.ds(chunk * D, D)
            load += [
                copies.start(src.at[pl.ds(0, ROWS), cols], ref.at[:, cols])
                for src, ref in zip((joint, joint_got), b)
            ]
        loads.append(load)
    done = []
    starts = parts_of(groups_vo, 384)
    for i, (lines, load) in enumerate(((v_lines, loads[0]), (o_lines, loads[1]))):
        cols = pl.ds(i * D, D)
        finish(load)
        done += columns_job(
            copies, lines, starts, 192, [ref.at[:, pl.ds((2 + i) * D, D)] for ref in b],
            [o.at[:, cols] for o in vo_outs], [v.at[:, cols] for v in vo_buffers], {},
            extra if i == 0 else None,
        )
    finish(loads[2])
    done += columns_job(
        copies, qk_lines, parts_of(groups_qk, 320), 160, b, qk_outs, qk_buffers, {}
    )
    finish(done)


VM = pl.BlockSpec(memory_space=pltpu.VMEM)
SM = pl.BlockSpec(memory_space=pltpu.SMEM)
HB = pl.BlockSpec(memory_space=pltpu.HBM)
LIMIT = 60 * 1024 * 1024


def call(kernel, ins, specs, outs, scratch, flops, moved):
    return pl.pallas_call(
        kernel,
        out_shape=tuple(
            (pltpu.HBM if o[2] is HB else jax.ShapeDtypeStruct)(*o[:2]) if isinstance(o, tuple) else o
            for o in outs
        ),
        in_specs=specs,
        out_specs=tuple(o[2] if isinstance(o, tuple) else VM for o in outs),
        scratch_shapes=scratch,
        compiler_params=pltpu.CompilerParams(vmem_limit_bytes=LIMIT),
        cost_estimate=pl.CostEstimate(flops=flops, bytes_accessed=moved, transcendentals=0),
    )(*ins)


def dma(n):
    return pltpu.SemaphoreType.DMA((n,))


TOKENS = ((ROWS, D), BF)
WIDE = ((ROWS, D), F32)
QKV = ((ROWS, 3 * D), BF)
PROB = ((20, 2 * SEQ, SEQ), BF)
HIDDEN = ((ROWS, FF), BF)
SUMS = ((2, D), F32)
ATT_W = pltpu.VMEM((D, 4 * D), BF)
UP_W = pltpu.VMEM((D, FF), BF)
DOWN_W = pltpu.VMEM((FF, D), BF)


def vmem(kind):
    return pltpu.VMEM(*kind)


def forward(ints, x, norms, weights):
    return call(
        forward_kernel,
        (ints, x, *norms, *weights),
        [SM] + [VM] * 5 + [HB] * 7,
        [TOKENS + (VM,)],
        [ATT_W, UP_W, DOWN_W]
        + [vmem(k) for k in (QKV, TOKENS, WIDE, TOKENS, TOKENS, HIDDEN)]
        + [dma(12)],
        6 * ROWS * D * FF, 40 * 2**20,
    )[0]


def both_ways(ints, x0, arriving, grad, norms, weights):
    kinds = (TOKENS, TOKENS, QKV, PROB, TOKENS, WIDE, TOKENS, HIDDEN, HIDDEN)
    return call(
        both_ways_kernel,
        (ints, x0, arriving, grad, *norms, *weights),
        [SM] + [VM] * 7 + [HB] * 7,
        [TOKENS + (VM,), TOKENS + (VM,)] + [k + (HB,) for k in kinds],
        [ATT_W, UP_W, DOWN_W] + [vmem(k) for k in kinds] + [vmem(WIDE), dma(12), dma(9)],
        12 * ROWS * D * FF, 60 * 2**20,
    )


def mlp_backward(ints, arriving, cot, slope, middle, g2, weights):
    return call(
        mlp_backward_kernel,
        (ints, arriving, cot, g2, slope, middle, *weights[2:]),
        [SM, VM, VM, VM] + [HB] * 7,
        [HIDDEN + (HB,), WIDE + (VM,), TOKENS + (VM,), SUMS + (VM,)],
        [
            UP_W, DOWN_W, vmem(TOKENS), vmem(WIDE), vmem(HIDDEN), vmem(WIDE), vmem(HIDDEN),
            dma(12), dma(17),
        ],
        2**20, 2**16,
    )


def heads_backward(ints, low, qkv, prob, weights):
    wout, oth = weights[1], weights[-1]
    return call(
        heads_backward_kernel,
        (ints, low, qkv, prob, wout, oth),
        [SM, VM] + [HB] * 4,
        [HIDDEN + (VM,)],
        [ATT_W, vmem(TOKENS), vmem(QKV), vmem(PROB), dma(4), dma(2)],
        2**20, 2**16,
    )[0]


def norm_one_backward(ints, g1, joint, dmiddle, x, weights):
    wqkv, oth = weights[0], weights[-1]
    return call(
        norm_one_backward_kernel,
        (ints, g1, joint, dmiddle, x, wqkv, oth),
        [SM, VM, VM] + [HB] * 4,
        [TOKENS + (VM,), SUMS + (VM,)],
        [ATT_W, vmem(WIDE), vmem(WIDE), vmem(TOKENS), dma(4), dma(2)],
        2**20, 2**16,
    )


def lay_out(h1, mixed, h2, active, indices):
    return call(
        lay_out_kernel,
        (h1, mixed, h2, active, *indices),
        [VM] * 7,
        [((LINES, ROWS), BF, VM), ((LINES, ROWS), BF, VM)],
        [pltpu.VMEM((1536, D), BF)],
        2**20, 2**16,
    )


def lines(count):
    return [pltpu.VMEM((count, ROWS), BF)] * 2


def up_down_grad(ints, groups, mine, got, du, du_got, grads):
    up, down = ((160, FF), BF), ((640, D), BF)
    outs = call(
        up_down_grad_kernel,
        (ints, groups[0], groups[1], mine, got, du, du_got, *grads),
        [SM] * 3 + [HB] * 8,
        [up + (HB,)] * 4 + [down + (HB,)] * 4,
        lines(640) + lines(2560) + [vmem(HIDDEN)] * 2 + [vmem(TOKENS)] * 2
        + [vmem(up)] * 4 + [vmem(down)] * 4 + [dma(40)],
        2**20, 2**16,
    )
    return outs[:4], outs[4:]


def attention_grad(groups, mine, got, joint, joint_got, extra):
    qk, vo = ((160, 2 * D), BF), ((192, 2 * D), BF)
    outs = call(
        attention_grad_kernel,
        (groups[0], groups[1], mine, got, joint, joint_got, extra),
        [SM] * 2 + [HB] * 4 + [VM],
        [qk + (HB,)] * 4 + [vo + (HB,)] * 4,
        lines(640) + lines(768) + lines(768) + [vmem(HIDDEN)] * 2
        + [vmem(qk)] * 4 + [vmem(vo)] * 4 + [dma(40)],
        2**20, 2**16,
    )
    return outs[:4], outs[4:]


def dp_pairs(move):
    pairs = []
    for z in range(4):
        for y in range(4):
            for c in range(2):
                to = move(z, y, c)
                pairs.append((z * 8 + y * 2 + c, to[0] * 8 + to[1] * 2 + to[2]))
    return pairs


FLIPS = {
    ("y", 1): dp_pairs(lambda z, y, c: (z, y ^ 1, c)),
    ("y", 3): dp_pairs(lambda z, y, c: (z, y ^ 3, c)),
    ("z", 1): dp_pairs(lambda z, y, c: (z ^ 1, y, c)),
    ("z", 3): dp_pairs(lambda z, y, c: (z ^ 3, y, c)),
}
CORE = dp_pairs(lambda z, y, c: (z, y, 1 - c))
SWAP = [(0, 1), (1, 0)]
ORDERS = ((0, 3, 1, 2), (0, 1, 2, 3))


def add_low(a, b):
    return (a.astype(F32) + b.astype(F32)).astype(BF)


def layout_rows(spacing, parity, core):
    order = ORDERS[parity]
    rows = []
    for c in (core, 1 - core):
        for p in range(2):
            for first in order:
                for second in order:
                    y, z = (first, second) if p == 0 else (second, first)
                    start = p * 640 + z * 160 + y * 40 + c * 20
                    rows += [start + i if i < 20 else -1 for i in range(spacing)]
    return np.array(rows, np.int32)


def block_rows(core):
    rows = []
    for c in (core, 1 - core):
        for block in range(8):
            rows += [block * 160 + c * 80 + i for i in range(80)]
    return np.array(rows, np.int32)


LAYOUTS = (
    (layout_rows(20, 0, 0), layout_rows(20, 0, 1)),
    (layout_rows(24, 1, 0), layout_rows(24, 1, 1)),
    (block_rows(0), block_rows(1)),
)


def picks_of(parity, at):
    if parity == 0:
        return jnp.where((at == 0) | (at == 3), 0, 1), at // 2
    return at // 2, at % 2


def flips_of(parity):
    return (1, 3) if parity == 0 else (3, 1)


class Flights:
    WINDOW = 5

    def __init__(self):
        self.gots = []

    def send(self, value, axis, flip):
        if len(self.gots) >= self.WINDOW:
            value, _ = lax.optimization_barrier((value, self.gots[-self.WINDOW]))
        got = (
            lax.ppermute(value, "pair", SWAP)
            if axis == "x"
            else lax.ppermute(value, "dp", FLIPS[axis, flip])
        )
        self.gots.append(got)
        return got


class Rings:
    def __init__(self, flights, send, keep, axes, parity, at):
        self.flights, self.to_send, self.keep = flights, send, keep
        self.plan = [
            (axis, flip, pick)
            for axis in axes
            for flip, pick in zip(flips_of(parity), picks_of(parity, at[axis]))
        ]
        self.step = 0

    def start(self):
        axis, flip, _ = self.plan[self.step]
        self.got = self.flights.send(self.to_send, axis, flip)
        self.step += 1

    def finish(self):
        value = add_low(self.keep, self.got)
        if self.step < 4:
            self.split(value)
        return value

    def finish_first(self):
        return add_low(self.keep, self.got)

    def split(self, value):
        pick = self.plan[self.step][2]
        half = value.shape[0] // 2
        self.to_send = lax.dynamic_slice_in_dim(value, (1 - pick) * half, half, 0)
        self.keep = lax.dynamic_slice_in_dim(value, pick * half, half, 0)


def join_up(up, qk):
    return jnp.concatenate([up, qk], axis=1)


def join_down(down, vo):
    return jnp.concatenate(
        [down.reshape(4, 80, D), vo[:, :D].reshape(4, 24, D), vo[:, D:].reshape(4, 24, D)], axis=1
    ).reshape(-1, D)


def over_pair(flights, values, pair):
    send = jnp.where(pair == 0, values[1], values[0])
    keep = jnp.where(pair == 0, values[0], values[1])
    return keep.astype(F32) + flights.send(send, "x", 1).astype(F32)


def sums_rows(sums):
    t = sums.reshape(4, 2, 4, 4, 2, 20)
    first = jnp.transpose(t[:, 0], (2, 1, 3, 0, 4)).reshape(1, 16, 1, 160)
    second = jnp.transpose(t[:, 1], (1, 2, 3, 0, 4)).reshape(1, 16, 1, 160)
    t = jnp.concatenate([first, second], axis=0)
    return jnp.pad(t, ((0, 0), (0, 0), (20, 3), (0, 96))).reshape(768, 256)


def shards(
    tokens, lengths, cotangent, w_qkv, w_out, w_up, w_down,
    norm1_gain, norm1_bias, norm2_gain, norm2_bias,
):
    section = lax.axis_index("section")
    pair = lax.axis_index("pair")
    place = lax.axis_index("dp")
    at = {"z": place // 8, "y": (place // 2) % 4}
    core = place % 2
    swap = lambda v: lax.ppermute(v, "dp", CORE)
    ints = jnp.concatenate(
        [
            pair[None].astype(jnp.int32), lengths[:, 0],
            section[None].astype(jnp.int32), core[None].astype(jnp.int32),
        ]
    )
    groups = [
        jnp.stack([1 - picks_of(k, at["y"])[0], 1 - picks_of(k, at["z"])[0]]).astype(jnp.int32)
        for k in range(2)
    ]
    indices = [jnp.where(core == 0, a, b)[:, None] for a, b in LAYOUTS]
    norms = (norm1_gain, norm1_bias, norm2_gain, norm2_bias)
    x0 = tokens.reshape(ROWS, D)
    cot = cotangent.reshape(ROWS, D)
    cot_got = swap(cot)
    wqkv, wout, wup, wdown = w_qkv[0], w_out[0], w_up[0], w_down[0]

    row = (place % 8) * PIECE
    att_piece = jnp.where(
        at["z"] == 3,
        lax.dynamic_slice(wout, (row, 0), (PIECE, D)),
        lax.dynamic_slice(wqkv, (row, jnp.minimum(at["z"], 2) * D), (PIECE, D)),
    )
    piece = jnp.concatenate(
        [
            att_piece,
            lax.dynamic_slice(wup, (row, at["z"] * D), (PIECE, D)),
            lax.dynamic_slice(wdown, (DIRECT + place * TAIL, 0), (TAIL, D)),
        ],
        axis=0,
    )
    piece = lax.ppermute(piece, "pair", SWAP)
    half = lax.dynamic_slice(wdown, (core * (DIRECT // 2), 0), (DIRECT // 2, D))
    half, piece = lax.optimization_barrier((half, piece))
    oth = lax.all_gather(piece, "dp", axis=0)
    near = lax.ppermute(half, "pair", SWAP)
    far = swap(near)

    ints, groups, indices, cot_got, oth, near, far = lax.optimization_barrier(
        (ints, groups, indices, cot_got, oth, near, far)
    )
    weights = (wqkv, wout, wup, wdown, near, far, oth)
    y = forward(ints, x0, norms, weights)
    arriving = lax.ppermute(y, "section", [(0, 1)])
    y, dx, x, h1, qkv, prob, mixed, middle, h2, active, slope = both_ways(
        ints, x0, arriving, cot, norms, weights
    )
    arriving = lax.ppermute(dx, "section", [(1, 0)])

    mine, send = lay_out(h1, mixed, h2, active, indices)
    arriving, send, mine = lax.optimization_barrier((arriving, send, mine))
    got = swap(send)
    arriving_got = swap(arriving)
    du, dmiddle, low, sums_two = mlp_backward(
        ints, arriving, cot, slope, middle, norm2_gain, weights
    )
    du, low, arriving_got, got = lax.optimization_barrier((du, low, arriving_got, got))
    grads = (arriving, cot, arriving_got, cot_got)
    du_got = swap(du)
    joint = heads_backward(ints, low, qkv, prob, weights)
    joint_got = swap(joint)
    joint, du, du_got, grads = lax.optimization_barrier((joint, du, du_got, grads))
    d_up, d_down = up_down_grad(ints, groups, mine, got, du, du_got, grads)
    joint, dmiddle, d_down = lax.optimization_barrier((joint, dmiddle, d_down))
    dx, sums_one = norm_one_backward(ints, norm1_gain, joint, dmiddle, x, weights)
    dx, sums_one, joint, joint_got, place, pair = lax.optimization_barrier(
        (dx, sums_one, joint, joint_got, place, pair)
    )
    at = {"z": place // 8, "y": (place // 2) % 4}
    extra = sums_rows(jnp.concatenate([sums_one, sums_two], axis=0))
    d_qk, d_vo = attention_grad(groups, mine, got, joint, joint_got, extra)
    keeps = [d[i] for d in (d_up, d_down, d_vo, d_qk) for i in (1, 3)]
    keeps = lax.optimization_barrier(keeps)
    d_up, d_down, d_vo, d_qk = (
        (d[0], keeps[2 * i], d[2], keeps[2 * i + 1])
        for i, d in enumerate((d_up, d_down, d_vo, d_qk))
    )

    flights = Flights()

    def rings(parts, parity):
        return [
            Rings(flights, parts[0], parts[1], "yz", parity, at),
            Rings(flights, parts[2], parts[3], "zy", parity, at),
        ]

    def each(method, group):
        return [getattr(r, method)() for r in group]

    down, up, vo, qk = rings(d_down, 1), rings(d_up, 0), rings(d_vo, 1), rings(d_qk, 0)
    def phase(now, later):
        each("start", now)
        gots, sends = lax.optimization_barrier(
            ([r.got for r in now], [r.to_send for r in later])
        )
        for r, v in zip(now, gots):
            r.got = v
        for r, v in zip(later, sends):
            r.to_send = v

    phase(down + up, vo + qk)
    each("finish", down + up)
    phase(vo + qk, down + up)
    each("finish", vo + qk)
    phase(down + up, vo + qk)
    each("start", vo + qk)
    for one, two, join in ((down, vo, join_down), (up, qk, join_up)):
        for a, b in zip(one, two):
            value = join(a.finish_first(), b.finish_first())
            a.split(value)
    each("start", down + up)
    each("finish", down + up)
    each("start", down + up)
    g_down = over_pair(flights, each("finish", down), pair)
    g_up = over_pair(flights, each("finish", up), pair)
    sums = g_down[100, :160].reshape(2, 80)
    sums = (
        lax.dynamic_index_in_dim(sums, place % 2, 0, keepdims=False)
        + swap(lax.dynamic_index_in_dim(sums, 1 - place % 2, 0, keepdims=False))
    ).reshape(4, 20)
    return (
        y.reshape(1, 2, 1, SEQ, D),
        dx.reshape(1, 2, 1, SEQ, D),
        jnp.concatenate([g_up[:, FF:], g_down[80:100]], axis=1)[None],
        g_down[104:124][None],
        g_up[:, :FF][None],
        g_down[:80][None],
        sums[0:1],
        sums[1:2],
        sums[2:3],
        sums[3:4],
    )


def solution(mesh):
    rows = ("pair", "dp")
    in_specs = (
        P(None, rows, None, None),
        P(None, rows),
        P(None, rows, None, None),
        P("section", "pair", None),
        P("section", "pair", None),
        P("section", "pair", None),
        P("section", "pair", None),
        P("section", None),
        P("section", None),
        P("section", None),
        P("section", None),
    )
    out_specs = (
        P("section", None, rows, None, None),
        P("section", None, rows, None, None),
        P("section", rows, None),
        P("section", rows, None),
        P("section", rows, None),
        P("section", rows, None),
        P("section", rows),
        P("section", rows),
        P("section", rows),
        P("section", rows),
    )
    return jax.shard_map(shards, mesh=mesh, in_specs=in_specs, out_specs=out_specs, check_vma=False)
```
